32 devices in a mesh: groups: 2 (over y), frame: 4 (over z), head: 2 (over x), sub: 2 (over core).
Axes of the slice: x: 2, y: 2, z: 4, core: 2. Of those that a mesh axis runs over, the one named last changes fastest.
Arguments:
- queries: bfloat16 [3072, 2560], P(('groups', 'frame'), ('head', 'sub')), parts along dimension 0, may hold values from -6 to 6, as said below
- keyvals: bfloat16 [2, 3072, 2560], P(None, ('groups', 'frame'), ('head', 'sub')), parts along dimension 1, may hold values from -6 to 6, as said below
- residual_in: float32 [3072, 5120], P(('groups', 'frame'), ('head', 'sub')), parts along dimension 0, may hold values from -3 to 3
- gate: float32 [10240], P(('groups', 'head', 'sub')), parts along dimension 0, may hold values from -4 to 4
- out_weight: bfloat16 [2560, 5120], P(('head', 'sub'), 'frame'), may hold values from -0.125 to 0.125
- pattern: int32 [48, 8], P(('groups', 'frame')), parts along dimension 0, may hold values from 0 to 23, as said below
- live: int32 [48], P(('groups', 'frame')), parts along dimension 0, may hold values from 4 to 8
Outputs:
- updated: float32 [3072, 5120], P(('groups', 'frame'), ('head', 'sub')), parts along dimension 0
The draws below stay inside these ranges and needn't reach their ends.
There are 2 independent parts, one for each index of `groups`. The reference program is written for one: setup_inputs(seed, part) draws one part's arguments, and reference() takes and returns one part's arrays. A program takes and returns all parts, laid end to end along the dimension named above; an argument that names none is the same for every part. Nothing has to cross between parts.
Inputs may be any that keep to these rules, and one draw needn't show every extreme that they name: `pattern`: entry 0 of each row is the query tile itself; entries below live of that row are distinct tiles lying in the query tile's frame or one frame before or after it; later entries repeat the query tile. `queries`: values of order one. `keyvals`: values of order one.
All inputs are finite; a program needn't handle non-finite values.
Results may differ from the reference program's by a relative error of at most 0.0065.
Values may be sent and summed in bfloat16 or wider, within the bound.
No kernel may reach another device: no remote copies, remote signals or barrier semaphores. Data moves between devices by JAX's collectives and lax.ppermute only.
A program may use at most 128 MiB of HBM per device.

```python
import math
import jax
import jax.numpy as jnp
from jax import lax

D = 5120
HEAD_DIM = 128
HEAD_DEV = 5
TILE = 64
TILES_F = 6
KSEL = 8
HEADS = 20
FRAMES = 4
TOKENS = 1536
N_HEAD = 2
N_SUB = 2


def base_field(key, salt):
    shape = (FRAMES * TILES_F * TILE, HEADS * HEAD_DIM)
    field = jnp.clip(jax.random.normal(jax.random.fold_in(key, salt), shape, jnp.float32), -5.0, 5.0)
    return field


def draw_queries(key, part):
    field = base_field(key, 21)
    return field.astype(jnp.bfloat16)


def draw_keyvals(key, part):
    keys = base_field(key, 22)
    values = base_field(key, 23)
    return jnp.stack([keys, values]).astype(jnp.bfloat16)


def tile_lists(key):
    tiles = FRAMES * TILES_F
    width = 3 * TILES_F
    own = jnp.arange(tiles, dtype=jnp.int32)
    own_frame = own // TILES_F
    own_spot = own % TILES_F
    column = jnp.arange(width, dtype=jnp.int32)
    cand_frame = own_frame[:, None] + column[None, :] // TILES_F - 1
    cand_spot = jnp.broadcast_to(column[None, :] % TILES_F, (tiles, width))
    valid = (cand_frame >= 0) & (cand_frame < FRAMES)
    is_self = (cand_frame == own_frame[:, None]) & (cand_spot == own_spot[:, None])
    noise = jax.random.randint(jax.random.fold_in(key, 31), (tiles, width), 0, 1 << 20)
    score = jnp.where(is_self, 1 << 29, jnp.where(valid, noise * width + column[None, :] + width, column[None, :] + 0 * noise))
    ranked, order = lax.top_k(score, KSEL)
    cand_id = cand_frame * TILES_F + cand_spot
    picked = jnp.take_along_axis(cand_id, order, axis=1)
    count = jnp.sum(valid.astype(jnp.int32), axis=1)
    wanted = jax.random.randint(jax.random.fold_in(key, 32), (tiles,), KSEL // 2, KSEL + 1)
    used = jnp.minimum(wanted, count)
    forced = jax.random.randint(jax.random.fold_in(key, 33), (), TILES_F, tiles - TILES_F)
    used = jnp.where(own == forced, KSEL, used)
    slot = jnp.arange(KSEL, dtype=jnp.int32)
    lists = jnp.where(slot[None, :] < used[:, None], picked, own[:, None])
    return (lists.astype(jnp.int32), used.astype(jnp.int32))


def draw_pattern(key, part):
    lists, used = tile_lists(key)
    return lists


def draw_live(key, part):
    lists, used = tile_lists(key)
    return used


def block_scale(key, dims, cuts, least, top_value):
    level = 1.0
    for dim, shards_of in cuts:
        draws = jax.random.uniform(jax.random.fold_in(jax.random.fold_in(key, 6), dim), (shards_of,), jnp.float32, least / len(cuts), top_value / len(cuts))
        level = level * jnp.repeat(jnp.exp(draws), dims[dim] // shards_of).reshape((-1,) + (1,) * (len(dims) - 1 - dim))
    return level


def bell_draw(key, shape, scale, bound, shards=(), kind=jnp.bfloat16):
    drawn = scale * jax.random.normal(key, shape, jnp.float32)
    if shards:
        drawn = drawn * block_scale(key, shape, shards, -0.22, 0.18)
    return jnp.clip(drawn, -bound, bound).astype(kind)


def setup_inputs(seed: int = 0, part: int = 0) -> dict:
    splits = jax.random.split(jax.random.key(seed), 8)
    own_keys = jax.random.split(jax.random.fold_in(splits[7], part), 8)
    queries = draw_queries(jax.random.fold_in(jax.random.fold_in(splits[7], part), 71), part)
    keyvals = draw_keyvals(jax.random.fold_in(jax.random.fold_in(splits[7], part), 71), part)
    residual_in = bell_draw(own_keys[2], (TOKENS, D), 0.5, 3.0, ((0, 4), (1, 4)), jnp.float32)
    gate = bell_draw(own_keys[3], (D,), 1.0, 4.0, ((0, 4),), jnp.float32)
    out_weight = bell_draw(splits[4], (HEADS * HEAD_DIM, D), (HEADS * HEAD_DIM) ** -0.5, 0.125, ((0, 4), (1, 4)))
    pattern = draw_pattern(jax.random.fold_in(jax.random.fold_in(splits[7], part), 71), part)
    live = draw_live(jax.random.fold_in(jax.random.fold_in(splits[7], part), 71), part)
    return {"queries": queries, "keyvals": keyvals, "residual_in": residual_in, "gate": gate, "out_weight": out_weight, "pattern": pattern, "live": live}


def attend_tile(tile_queries, key_rows, value_rows, count):
    scores = jnp.einsum('qhd,khd->hqk', tile_queries.astype(jnp.float32), key_rows.astype(jnp.float32)) * (1.0 / math.sqrt(HEAD_DIM))
    slot = jnp.arange(KSEL * TILE, dtype=jnp.int32) // TILE
    scores = jnp.where((slot < count)[None, None, :], scores, -1e+30)
    row_max = lax.optimization_barrier(jnp.max(scores, axis=-1, keepdims=True))
    expo = jnp.exp(scores - row_max)
    probs = (expo / lax.optimization_barrier(jnp.sum(expo, axis=-1, keepdims=True))).astype(jnp.bfloat16)
    return jnp.einsum('hqk,khd->qhd', probs.astype(jnp.float32), value_rows.astype(jnp.float32)).astype(jnp.bfloat16)

def reference(queries, keyvals, residual_in, gate, out_weight, pattern, live):
    tiles = FRAMES * TILES_F
    query_tiles = queries.reshape(tiles, TILE, HEADS, HEAD_DIM)
    key_tiles = keyvals[0].reshape(tiles, TILE, HEADS, HEAD_DIM)
    value_tiles = keyvals[1].reshape(tiles, TILE, HEADS, HEAD_DIM)

    def one_tile(packed):
        tile_queries, listed, count = packed
        key_rows = key_tiles[listed].reshape(KSEL * TILE, HEADS, HEAD_DIM)
        value_rows = value_tiles[listed].reshape(KSEL * TILE, HEADS, HEAD_DIM)
        return attend_tile(tile_queries, key_rows, value_rows, count)
    attended = lax.map(one_tile, (query_tiles, pattern, live))
    attended = attended.reshape(tiles * TILE, HEADS * HEAD_DIM)
    group_width = HEAD_DEV * HEAD_DIM

    def add_group(total, group):
        start = (group * group_width).astype(jnp.int32)
        columns = lax.dynamic_slice_in_dim(attended, start, group_width, 1)
        weights = lax.dynamic_slice_in_dim(out_weight, start, group_width, 0)
        term = jnp.dot(columns, weights, preferred_element_type=jnp.float32).astype(jnp.bfloat16)
        term = lax.optimization_barrier(term)
        return (total + term.astype(jnp.float32), None)
    empty = jnp.zeros((tiles * TILE, D), jnp.float32)
    projected, _ = lax.scan(add_group, empty, jnp.arange(N_HEAD * N_SUB, dtype=jnp.int32))
    return residual_in + gate[None, :] * projected
```

```python
import math

import jax
import jax.numpy as jnp
from jax import lax
from jax.experimental import pallas as pl
from jax.experimental.pallas import tpu as pltpu
from jax.sharding import PartitionSpec as P

HEAD_DIM = 128
TILES_F = 6
KSEL = 8
AXES = ("groups", "frame", "head", "sub")
MIB = 1 << 20


def attend_kernel(ids, live, q_ref, own_ref, low_ref, high_ref, out_ref, kv, sems):
    tiles = ids.shape[0]
    rows, width = q_ref.shape
    tile = rows // tiles
    heads = width // HEAD_DIM
    copies = [
        pltpu.make_async_copy(src, kv.at[:, pl.ds(i * rows, rows), :], sems.at[i])
        for i, src in enumerate((low_ref, own_ref, high_ref))
    ]
    for copy in copies:
        copy.start()
    for copy in copies:
        copy.wait()
    scale = 1.0 / math.sqrt(HEAD_DIM)
    column = lax.broadcasted_iota(jnp.int32, (tile, KSEL * tile), 1)

    def one_tile(t, carry):
        row = pl.multiple_of(t * tile, tile)
        starts = [pl.multiple_of(ids[t, s] * tile, tile) for s in range(KSEL)]
        allowed = column < live[t] * tile
        for h in range(heads):
            lanes = slice(h * HEAD_DIM, (h + 1) * HEAD_DIM)
            keys = jnp.concatenate([kv[0, pl.ds(s, tile), lanes] for s in starts], axis=0)
            values = jnp.concatenate([kv[1, pl.ds(s, tile), lanes] for s in starts], axis=0)
            scores = lax.dot_general(
                q_ref[pl.ds(row, tile), lanes],
                keys,
                (((1,), (1,)), ((), ())),
                preferred_element_type=jnp.float32,
            )
            scores = jnp.where(allowed, scores * scale, -1e30)
            expo = jnp.exp(scores - jnp.max(scores, axis=-1, keepdims=True))
            probs = (expo / jnp.sum(expo, axis=-1, keepdims=True)).astype(jnp.bfloat16)
            out_ref[pl.ds(row, tile), lanes] = jnp.dot(
                probs, values, preferred_element_type=jnp.float32
            ).astype(jnp.bfloat16)
        return carry

    lax.fori_loop(0, tiles, one_tile, 0)


def attend(queries, keyvals, low, high, pattern, live):
    rows, width = queries.shape
    tile_count = pattern.shape[0]
    local_ids = pattern - (lax.axis_index("frame") * tile_count - TILES_F)
    anywhere = pl.BlockSpec(memory_space=pl.ANY)
    scalars = pl.BlockSpec(memory_space=pltpu.SMEM)
    whole = pl.BlockSpec(memory_space=pltpu.VMEM)
    return pl.pallas_call(
        attend_kernel,
        out_shape=jax.ShapeDtypeStruct((rows, width), jnp.bfloat16),
        in_specs=[scalars, scalars, whole, anywhere, anywhere, anywhere],
        out_specs=whole,
        scratch_shapes=[
            pltpu.VMEM((2, 3 * rows, width), jnp.bfloat16),
            pltpu.SemaphoreType.DMA((3,)),
        ],
        compiler_params=pltpu.CompilerParams(vmem_limit_bytes=24 * MIB),
        cost_estimate=pl.CostEstimate(
            flops=4 * rows * KSEL * rows // tile_count * width,
            bytes_accessed=16 * rows * width,
            transcendentals=rows * KSEL * rows // tile_count * (width // HEAD_DIM),
        ),
        name="attend",
    )(local_ids, live, queries, keyvals, low, high)


def halos(keyvals):
    count = lax.axis_size("frame")
    forward = [(i, i + 1) for i in range(count - 1)]
    backward = [(b, a) for a, b in forward]
    return lax.ppermute(keyvals, "frame", forward), lax.ppermute(keyvals, "frame", backward)


def plain(queries, keyvals, residual_in, gate, out_weight, pattern, live):
    low, high = halos(keyvals)
    attended = attend(queries, keyvals, low, high, pattern, live)
    weights = lax.all_gather(out_weight, "frame", axis=1, tiled=True)
    partial_rows = jnp.dot(attended, weights, preferred_element_type=jnp.float32)
    summed = lax.psum_scatter(
        partial_rows.astype(jnp.bfloat16), ("head", "sub"), scatter_dimension=1, tiled=True
    ).astype(jnp.float32)
    return residual_in + gate[None, :] * summed


def place(y, f, x, c):
    return ((y * 4 + f) * 2 + x) * 2 + c


def pairs(move, keep=lambda y, f, x, c: True):
    found = []
    for y in range(2):
        for f in range(4):
            for x in range(2):
                for c in range(2):
                    if keep(y, f, x, c):
                        found.append((place(y, f, x, c), place(*move(y, f, x, c))))
    return found


def block_at(k, f, x):
    return (f - k) % 4 if x == 0 else (f + k) % 4


def to_owner(steps, cross):
    def move(y, f, x, c):
        g = block_at(steps[x], f, x)
        return c, f, g // 2, g % 2

    return pairs(move, lambda y, f, x, c: (y ^ c) == cross)


def send(array, route):
    return lax.ppermute(array, AXES, route)


def finish_kernel(spot, *refs):
    direct, crossed = refs[:4], refs[4:8]
    residual, gate, out = refs[8:]
    half = direct[0].shape[1]
    for cross, parts in ((0, direct), (1, crossed)):
        start = pl.multiple_of((spot[0] ^ cross) * half, half)
        lanes = pl.ds(start, half)
        total = parts[0][...].astype(jnp.float32)
        for part in parts[1:]:
            total = total + part[...].astype(jnp.float32)
        out[:, lanes] = residual[:, lanes] + gate[:, lanes] * total


def finish(direct, crossed, residual_in, gate, spot):
    rows, width = residual_in.shape
    step = 128
    narrow = pl.BlockSpec((step, width // 2), lambda i: (i, 0))
    wide = pl.BlockSpec((step, width), lambda i: (i, 0))
    return pl.pallas_call(
        finish_kernel,
        grid=(rows // step,),
        out_shape=jax.ShapeDtypeStruct((rows, width), jnp.float32),
        in_specs=[pl.BlockSpec(memory_space=pltpu.SMEM)]
        + [narrow] * 8
        + [wide, pl.BlockSpec((1, width), lambda i: (0, 0))],
        out_specs=wide,
        compiler_params=pltpu.CompilerParams(vmem_limit_bytes=32 * MIB),
        name="finish",
    )(spot, *direct, *crossed, residual_in, gate[None, :])


def ringed(queries, keyvals, residual_in, gate, out_weight, pattern, live):
    y = lax.axis_index("groups")
    x = lax.axis_index("head")
    c = lax.axis_index("sub")
    columns = out_weight.shape[1] // 2
    low, high = halos(keyvals)

    ring = pairs(lambda y, f, x, c: (y, (f + 1) % 4 if x == 0 else (f - 1) % 4, x, c))
    sibling = pairs(lambda y, f, x, c: (y, f, x, 1 - c))
    mine = lax.dynamic_slice_in_dim(out_weight, y * columns, columns, axis=1)
    held = [mine]
    for _ in range(3):
        held.append(send(held[-1], ring))
    other = [send(w, sibling) for w in held]

    attended = attend(queries, keyvals, low, high, pattern, live)
    first = send(
        attended,
        pairs(lambda y, f, x, c: (1 - y, f, x, c) if c == y else (y, f, x, 1 - c)),
    )
    second = send(
        attended,
        pairs(lambda y, f, x, c: (1 - y, f, x, 1 - c), lambda y, f, x, c: c != y),
    )
    here = y == c
    rows_own = jnp.where(here, attended, first)
    rows_sib = jnp.where(here, first, second)

    def sums(k):
        total = jnp.dot(rows_own, held[k], preferred_element_type=jnp.float32)
        total = total + jnp.dot(rows_sib, other[k], preferred_element_type=jnp.float32)
        return total.astype(jnp.bfloat16)

    s0, s1, s2, s3 = [sums(k) for k in range(4)]
    left = x == 0
    mixed = (jnp.where(left, s0, s2), jnp.where(left, s2, s0))
    direct, crossed = [], []
    for array, steps in ((s1, (1, 1)), (mixed[0], (0, 2)), (mixed[1], (2, 0)), (s3, (3, 3))):
        direct.append(send(array, to_owner(steps, 0)))
        crossed.append(send(array, to_owner(steps, 1)))
    return finish(direct, crossed, residual_in, gate, jnp.reshape(y, (1,)))


def solution(mesh):
    sizes = tuple(mesh.shape[axis] for axis in AXES)
    in_specs = (
        P(("groups", "frame"), ("head", "sub")),
        P(None, ("groups", "frame"), ("head", "sub")),
        P(("groups", "frame"), ("head", "sub")),
        P(("groups", "head", "sub")),
        P(("head", "sub"), "frame"),
        P(("groups", "frame"), None),
        P(("groups", "frame")),
    )
    return jax.shard_map(
        ringed if sizes == (2, 4, 2, 2) else plain,
        mesh=mesh,
        in_specs=in_specs,
        out_specs=P(("groups", "frame"), ("head", "sub")),
        check_vma=False,
    )
```

```python
import math

import jax
import jax.numpy as jnp
from jax import lax
from jax.experimental import pallas as pl
from jax.experimental.pallas import tpu as pltpu
from jax.sharding import PartitionSpec as P

HEAD_DIM = 128
TILES_F = 6
KSEL = 8
AXES = ("groups", "frame", "head", "sub")
MIB = 1 << 20


def attend_kernel(ids, live, q_ref, own_ref, low_ref, high_ref, out_ref, kv, sems):
    tiles = ids.shape[0]
    rows, width = q_ref.shape
    tile = rows // tiles
    heads = width // HEAD_DIM
    copies = [
        pltpu.make_async_copy(src, kv.at[:, pl.ds(i * rows, rows), :], sems.at[i])
        for i, src in enumerate((low_ref, own_ref, high_ref))
    ]
    for copy in copies:
        copy.start()
    for copy in copies:
        copy.wait()
    scale = math.log2(math.e) / math.sqrt(HEAD_DIM)
    key_row = lax.broadcasted_iota(jnp.int32, (KSEL * tile, 1), 0)
    lanes = [slice(h * HEAD_DIM, (h + 1) * HEAD_DIM) for h in range(heads)]

    def one_tile(t, carry):
        row = pl.multiple_of(t * tile, tile)
        starts = [pl.multiple_of(ids[t, s] * tile, tile) for s in range(KSEL)]

        def listed(which, lane):
            return jnp.concatenate([kv[which, pl.ds(s, tile), lane] for s in starts], axis=0)

        scores = jnp.concatenate(
            [
                lax.dot_general(
                    listed(0, lane),
                    q_ref[pl.ds(row, tile), lane],
                    (((1,), (1,)), ((), ())),
                    preferred_element_type=jnp.float32,
                )
                for lane in lanes
            ],
            axis=1,
        )
        scores = jnp.where(key_row < live[t] * tile, scores * scale, -1e30)
        expo = jnp.exp2(scores - jnp.max(scores, axis=0, keepdims=True))
        probs = (expo * (1.0 / jnp.sum(expo, axis=0, keepdims=True))).astype(jnp.bfloat16)
        for h, lane in enumerate(lanes):
            out_ref[pl.ds(row, tile), lane] = lax.dot_general(
                probs[:, h * tile : (h + 1) * tile],
                listed(1, lane),
                (((0,), (0,)), ((), ())),
                preferred_element_type=jnp.float32,
            ).astype(jnp.bfloat16)
        return carry

    lax.fori_loop(0, tiles, one_tile, 0)


def attend(queries, keyvals, low, high, pattern, live):
    rows, width = queries.shape
    tile_count = pattern.shape[0]
    local_ids = pattern - (lax.axis_index("frame") * tile_count - TILES_F)
    local_ids = jnp.clip(local_ids, 0, 3 * tile_count - 1)
    anywhere = pl.BlockSpec(memory_space=pl.ANY)
    scalars = pl.BlockSpec(memory_space=pltpu.SMEM)
    whole = pl.BlockSpec(memory_space=pltpu.VMEM)
    return pl.pallas_call(
        attend_kernel,
        out_shape=jax.ShapeDtypeStruct((rows, width), jnp.bfloat16),
        in_specs=[scalars, scalars, whole, anywhere, anywhere, anywhere],
        out_specs=whole,
        scratch_shapes=[
            pltpu.VMEM((2, 3 * rows, width), jnp.bfloat16),
            pltpu.SemaphoreType.DMA((3,)),
        ],
        compiler_params=pltpu.CompilerParams(vmem_limit_bytes=24 * MIB),
        cost_estimate=pl.CostEstimate(flops=1, bytes_accessed=1, transcendentals=0),
        name="attend",
    )(local_ids, live, queries, keyvals, low, high)


def halos(keyvals):
    count = lax.axis_size("frame")
    forward = [(i, i + 1) for i in range(count - 1)]
    backward = [(b, a) for a, b in forward]
    return lax.ppermute(keyvals, "frame", forward), lax.ppermute(keyvals, "frame", backward)


def plain(queries, keyvals, residual_in, gate, out_weight, pattern, live):
    low, high = halos(keyvals)
    attended = attend(queries, keyvals, low, high, pattern, live)
    weights = lax.all_gather(out_weight, "frame", axis=1, tiled=True)
    partial_rows = jnp.dot(attended, weights, preferred_element_type=jnp.float32)
    summed = lax.psum_scatter(
        partial_rows.astype(jnp.bfloat16), ("head", "sub"), scatter_dimension=1, tiled=True
    ).astype(jnp.float32)
    return residual_in + gate[None, :] * summed


def place(y, f, x, c):
    return ((y * 4 + f) * 2 + x) * 2 + c


def pairs(move, keep=lambda y, f, x, c: True):
    found = []
    for y in range(2):
        for f in range(4):
            for x in range(2):
                for c in range(2):
                    if keep(y, f, x, c):
                        found.append((place(y, f, x, c), place(*move(y, f, x, c))))
    return found


def block_at(k, f, x):
    return (f - k) % 4 if x == 0 else (f + k) % 4


def to_owner(steps, crosses):
    def move(y, f, x, c):
        g = block_at(steps[y ^ c][x], f, x)
        return c, f, g // 2, g % 2

    return pairs(move, lambda y, f, x, c: (y ^ c) in crosses)


def send(array, route, name):
    with jax.named_scope(name):
        return lax.ppermute(array, AXES, route)


def after(value, *earlier):
    return lax.optimization_barrier((value, *earlier))[0]


def finish_kernel(spot, *refs):
    residual, gate, out = refs[-3:]
    half = residual.shape[1] // 2
    count = (len(refs) - 3) // 2
    for cross, parts in ((0, refs[:count]), (1, refs[count : 2 * count])):
        lanes = pl.ds(pl.multiple_of((spot[0] ^ cross) * half, half), half)
        total = parts[0][...].astype(jnp.float32)
        for part in parts[1:]:
            total = total + part[...].astype(jnp.float32)
        out[:, lanes] = residual[:, lanes] + gate[:, lanes] * total


def finish(direct, crossed, residual_in, gate, spot):
    rows, width = residual_in.shape
    step = 128
    parts = [pl.BlockSpec((step, part.shape[1]), lambda i: (i, 0)) for part in direct + crossed]
    wide = pl.BlockSpec((step, width), lambda i: (i, 0))
    return pl.pallas_call(
        finish_kernel,
        grid=(rows // step,),
        out_shape=jax.ShapeDtypeStruct((rows, width), jnp.float32),
        in_specs=[pl.BlockSpec(memory_space=pltpu.SMEM)]
        + parts
        + [wide, pl.BlockSpec((1, width), lambda i: (0, 0))],
        out_specs=wide,
        compiler_params=pltpu.CompilerParams(vmem_limit_bytes=32 * MIB),
        name="finish",
    )(spot, *direct, *crossed, residual_in, gate[None, :])


def ringed(queries, keyvals, residual_in, gate, out_weight, pattern, live):
    y = lax.axis_index("groups")
    x = lax.axis_index("head")
    c = lax.axis_index("sub")
    half = out_weight.shape[1] // 2
    low, high = halos(keyvals)

    ring = pairs(lambda y, f, x, c: (y, (f + 1) % 4 if x == 0 else (f - 1) % 4, x, c))
    here = y == c
    left = x == 0

    def sums(weights, name):
        def product(rows):
            return jnp.dot(rows, weights, preferred_element_type=jnp.float32)

        swapped = send(
            product(given).astype(jnp.bfloat16),
            pairs(lambda y, f, x, c: (y, f, x, 1 - c)),
            "core_swap_" + name,
        )
        return (product(kept) + swapped.astype(jnp.float32)).astype(jnp.bfloat16)

    def to_owners(array, steps, name):
        return [
            send(array, to_owner((steps,) * 2, (0,)), "sums_" + name),
            send(array, to_owner((steps,) * 2, (1,)), "sums_cross_" + name),
        ]

    w0 = lax.dynamic_slice_in_dim(out_weight, y * half, half, axis=1)
    w1 = send(after(w0, low), ring, "ring_1")
    attended = attend(queries, keyvals, low, high, pattern, live)
    w2 = send(w1, ring, "ring_2")
    others = send(attended, pairs(lambda y, f, x, c: (1 - y, f, x, c)), "rows_of_other_group")
    kept = jnp.where(here, attended, others)
    given = jnp.where(here, others, attended)
    s1 = sums(w1, "1")
    middle = to_owners(s1, (1, 1), "1")
    s0 = sums(w0, "0")
    w2 = after(w2, s0, s1)
    w3 = send(w2, ring, "ring_3")
    w2, *middle = lax.optimization_barrier((w2, *middle))
    s2 = sums(w2, "2")
    low_sum, high_sum = jnp.where(left, s0, s2), jnp.where(left, s2, s0)
    early = to_owners(low_sum, (0, 2), "02") + to_owners(high_sum, (2, 0), "20")
    w3, *early = lax.optimization_barrier((w3, *early))
    s3 = sums(w3, "3")
    last = to_owners(s3, (3, 3), "3")
    return finish(
        [middle[0], early[0], early[2], last[0]],
        [middle[1], early[1], early[3], last[1]],
        residual_in,
        gate,
        jnp.reshape(y, (1,)),
    )


def solution(mesh):
    sizes = tuple(mesh.shape[axis] for axis in AXES)
    in_specs = (
        P(("groups", "frame"), ("head", "sub")),
        P(None, ("groups", "frame"), ("head", "sub")),
        P(("groups", "frame"), ("head", "sub")),
        P(("groups", "head", "sub")),
        P(("head", "sub"), "frame"),
        P(("groups", "frame"), None),
        P(("groups", "frame")),
    )
    return jax.shard_map(
        ringed if sizes == (2, 4, 2, 2) else plain,
        mesh=mesh,
        in_specs=in_specs,
        out_specs=P(("groups", "frame"), ("head", "sub")),
        check_vma=False,
    )
```

```python
import math

import jax
import jax.numpy as jnp
from jax import lax
from jax.experimental import pallas as pl
from jax.experimental.pallas import tpu as pltpu
from jax.sharding import PartitionSpec as P

HEAD_DIM = 128
TILES_F = 6
KSEL = 8
AXES = ("groups", "frame", "head", "sub")
MIB = 1 << 20


def weight(microseconds):
    return pl.CostEstimate(
        flops=int(microseconds * 1e9), bytes_accessed=int(microseconds * 3e6), transcendentals=0
    )


def fence_kernel(token, out):
    out[0] = token[0]


def fence(token, *arrays):
    *arrays, token = lax.optimization_barrier((*arrays, token))
    scalar = pl.BlockSpec(memory_space=pltpu.SMEM)
    token = pl.pallas_call(
        fence_kernel,
        out_shape=jax.ShapeDtypeStruct((1,), jnp.int32),
        in_specs=[scalar],
        out_specs=scalar,
        cost_estimate=weight(50),
        name="fence",
    )(token)
    return (*arrays, token)


def attend_kernel(ids, live, q_ref, own_ref, low_ref, high_ref, out_ref, kv, sems):
    tiles = ids.shape[0]
    rows, width = q_ref.shape
    tile = rows // tiles
    heads = width // HEAD_DIM
    copies = [
        pltpu.make_async_copy(src, kv.at[:, pl.ds(i * rows, rows), :], sems.at[i])
        for i, src in enumerate((low_ref, own_ref, high_ref))
    ]
    for copy in copies:
        copy.start()
    for copy in copies:
        copy.wait()
    scale = math.log2(math.e) / math.sqrt(HEAD_DIM)
    key_row = lax.broadcasted_iota(jnp.int32, (KSEL * tile, 1), 0)
    lanes = [slice(h * HEAD_DIM, (h + 1) * HEAD_DIM) for h in range(heads)]

    def one_tile(t, carry):
        row = pl.multiple_of(t * tile, tile)
        starts = [pl.multiple_of(ids[t, s] * tile, tile) for s in range(KSEL)]

        def listed(which, lane):
            return jnp.concatenate([kv[which, pl.ds(s, tile), lane] for s in starts], axis=0)

        scores = jnp.concatenate(
            [
                lax.dot_general(
                    listed(0, lane),
                    q_ref[pl.ds(row, tile), lane],
                    (((1,), (1,)), ((), ())),
                    preferred_element_type=jnp.float32,
                )
                for lane in lanes
            ],
            axis=1,
        )
        scores = jnp.where(key_row < live[t] * tile, scores * scale, -1e30)
        expo = jnp.exp2(scores - jnp.max(scores, axis=0, keepdims=True))
        probs = (expo * (1.0 / jnp.sum(expo, axis=0, keepdims=True))).astype(jnp.bfloat16)
        for h, lane in enumerate(lanes):
            out_ref[pl.ds(row, tile), lane] = lax.dot_general(
                probs[:, h * tile : (h + 1) * tile],
                listed(1, lane),
                (((0,), (0,)), ((), ())),
                preferred_element_type=jnp.float32,
            ).astype(jnp.bfloat16)
        return carry

    lax.fori_loop(0, tiles, one_tile, 0)


def attend(queries, keyvals, low, high, pattern, live):
    rows, width = queries.shape
    tile_count = pattern.shape[0]
    local_ids = pattern - (lax.axis_index("frame") * tile_count - TILES_F)
    local_ids = jnp.clip(local_ids, 0, 3 * tile_count - 1)
    anywhere = pl.BlockSpec(memory_space=pl.ANY)
    scalars = pl.BlockSpec(memory_space=pltpu.SMEM)
    whole = pl.BlockSpec(memory_space=pltpu.VMEM)
    return pl.pallas_call(
        attend_kernel,
        out_shape=jax.ShapeDtypeStruct((rows, width), jnp.bfloat16),
        in_specs=[scalars, scalars, whole, anywhere, anywhere, anywhere],
        out_specs=whole,
        scratch_shapes=[
            pltpu.VMEM((2, 3 * rows, width), jnp.bfloat16),
            pltpu.SemaphoreType.DMA((3,)),
        ],
        compiler_params=pltpu.CompilerParams(vmem_limit_bytes=24 * MIB),
        cost_estimate=weight(8),
        name="attend",
    )(local_ids, live, queries, keyvals, low, high)


def halos(keyvals):
    count = lax.axis_size("frame")
    forward = [(i, i + 1) for i in range(count - 1)]
    backward = [(b, a) for a, b in forward]
    return lax.ppermute(keyvals, "frame", forward), lax.ppermute(keyvals, "frame", backward)


def plain(queries, keyvals, residual_in, gate, out_weight, pattern, live):
    low, high = halos(keyvals)
    attended = attend(queries, keyvals, low, high, pattern, live)
    weights = lax.all_gather(out_weight, "frame", axis=1, tiled=True)
    partial_rows = jnp.dot(attended, weights, preferred_element_type=jnp.float32)
    summed = lax.psum_scatter(
        partial_rows.astype(jnp.bfloat16), ("head", "sub"), scatter_dimension=1, tiled=True
    ).astype(jnp.float32)
    return residual_in + gate[None, :] * summed


def place(y, f, x, c):
    return ((y * 4 + f) * 2 + x) * 2 + c


def pairs(move, keep=lambda y, f, x, c: True):
    found = []
    for y in range(2):
        for f in range(4):
            for x in range(2):
                for c in range(2):
                    if keep(y, f, x, c):
                        found.append((place(y, f, x, c), place(*move(y, f, x, c))))
    return found


def block_at(k, f, x):
    return (f - k) % 4 if x == 0 else (f + k) % 4


def to_owner(steps, crosses):
    def move(y, f, x, c):
        g = block_at(steps[y ^ c][x], f, x)
        return c, f, g // 2, g % 2

    return pairs(move, lambda y, f, x, c: (y ^ c) in crosses)


def send(array, route, name):
    with jax.named_scope(name):
        return lax.ppermute(array, AXES, route)


def after(value, *earlier):
    return lax.optimization_barrier((value, *earlier))[0]


def finish_kernel(spot, *refs):
    residual, gate, out = refs[-3:]
    half = residual.shape[1] // 2
    count = (len(refs) - 3) // 2
    for cross, parts in ((0, refs[:count]), (1, refs[count : 2 * count])):
        lanes = pl.ds(pl.multiple_of((spot[0] ^ cross) * half, half), half)
        total = parts[0][...].astype(jnp.float32)
        for part in parts[1:]:
            total = total + part[...].astype(jnp.float32)
        out[:, lanes] = residual[:, lanes] + gate[:, lanes] * total


def finish(direct, crossed, residual_in, gate, spot):
    rows, width = residual_in.shape
    step = 128
    parts = [pl.BlockSpec((step, part.shape[1]), lambda i: (i, 0)) for part in direct + crossed]
    wide = pl.BlockSpec((step, width), lambda i: (i, 0))
    return pl.pallas_call(
        finish_kernel,
        grid=(rows // step,),
        out_shape=jax.ShapeDtypeStruct((rows, width), jnp.float32),
        in_specs=[pl.BlockSpec(memory_space=pltpu.SMEM)]
        + parts
        + [wide, pl.BlockSpec((1, width), lambda i: (0, 0))],
        out_specs=wide,
        compiler_params=pltpu.CompilerParams(vmem_limit_bytes=32 * MIB),
        name="finish",
    )(spot, *direct, *crossed, residual_in, gate[None, :])


def ringed(queries, keyvals, residual_in, gate, out_weight, pattern, live):
    y = lax.axis_index("groups")
    x = lax.axis_index("head")
    c = lax.axis_index("sub")
    half = out_weight.shape[1] // 2
    tie = lax.optimization_barrier

    ring = pairs(lambda y, f, x, c: (y, (f + 1) % 4 if x == 0 else (f - 1) % 4, x, c))
    sibling = pairs(lambda y, f, x, c: (y, f, x, 1 - c))
    here = y == c
    left = x == 0

    def to_owners(array, steps, name):
        return [
            send(array, to_owner((steps,) * 2, (0,)), "sums_" + name),
            send(array, to_owner((steps,) * 2, (1,)), "sums_cross_" + name),
        ]

    low, high = halos(keyvals)
    w0 = lax.dynamic_slice_in_dim(out_weight, y * half, half, axis=1)
    v0 = send(w0, sibling, "core_swap_0")
    w0, v0, low, high = tie((w0, v0, low, high))
    w1 = send(w0, ring, "ring_1")
    attended = attend(queries, keyvals, low, high, pattern, live)
    first = send(
        attended,
        pairs(lambda y, f, x, c: (1 - y, f, x, c) if c == y else (y, f, x, 1 - c)),
        "rows_1",
    )
    second = send(
        attended,
        pairs(lambda y, f, x, c: (1 - y, f, x, 1 - c), lambda y, f, x, c: c != y),
        "rows_2",
    )

    def region(token, body, *operands):
        shapes = jax.eval_shape(body, *operands)
        return lax.cond(
            token[0] > 0,
            body,
            lambda *_: jax.tree.map(lambda leaf: jnp.zeros(leaf.shape, leaf.dtype), shapes),
            *operands,
        )

    def sums(rows_own, rows_sib, own, sib):
        total = jnp.dot(rows_own, own, preferred_element_type=jnp.float32)
        total = total + jnp.dot(rows_sib, sib, preferred_element_type=jnp.float32)
        return total.astype(jnp.bfloat16)

    def swapped(w):
        return send(w, sibling, "core_swap")

    def begin(rows_own, rows_sib, w1):
        return sums(rows_own, rows_sib, w1, swapped(w1))

    def mix(rows_own, rows_sib, s0, w2):
        s2 = sums(rows_own, rows_sib, w2, swapped(w2))
        return jnp.where(left, s0, s2), jnp.where(left, s2, s0)

    def end(rows_own, rows_sib, w3):
        return sums(rows_own, rows_sib, w3, swapped(w3))

    w2 = send(w1, ring, "ring_2")
    w1, token = fence(live[:1], w1)
    first, second, token = tie((first, second, token))
    rows_own = jnp.where(here, attended, first)
    rows_sib = jnp.where(here, first, second)
    s1 = region(token, begin, rows_own, rows_sib, w1)
    middle = to_owners(s1, (1, 1), "1")
    s0 = region(token, sums, rows_own, rows_sib, w0, v0)
    w2, s0 = tie((w2, s0))
    w3 = send(w2, ring, "ring_3")
    w2, *middle = tie((w2, *middle))
    low_sum, high_sum = region(token, mix, rows_own, rows_sib, s0, w2)
    early = to_owners(low_sum, (0, 2), "02") + to_owners(high_sum, (2, 0), "20")
    w3, low_sum, high_sum = tie((w3, low_sum, high_sum))
    s3 = region(token, end, rows_own, rows_sib, w3)
    s3, *early = tie((s3, *early))
    middle += early
    last = to_owners(s3, (3, 3), "3")
    spot = jnp.reshape(y, (1,))
    base = finish(middle[::2], middle[1::2], residual_in, gate, spot)
    return finish(last[::2], last[1::2], base, gate, spot)


def solution(mesh):
    sizes = tuple(mesh.shape[axis] for axis in AXES)
    in_specs = (
        P(("groups", "frame"), ("head", "sub")),
        P(None, ("groups", "frame"), ("head", "sub")),
        P(("groups", "frame"), ("head", "sub")),
        P(("groups", "head", "sub")),
        P(("head", "sub"), "frame"),
        P(("groups", "frame"), None),
        P(("groups", "frame")),
    )
    return jax.shard_map(
        ringed if sizes == (2, 4, 2, 2) else plain,
        mesh=mesh,
        in_specs=in_specs,
        out_specs=P(("groups", "frame"), ("head", "sub")),
        check_vma=False,
    )
```

```python
import math

import jax
import jax.numpy as jnp
from jax import lax
from jax.experimental import pallas as pl
from jax.experimental.pallas import tpu as pltpu
from jax.sharding import PartitionSpec as P

HEAD_DIM = 128
TILES_F = 6
KSEL = 8
AXES = ("groups", "frame", "head", "sub")
MIB = 1 << 20


def weight(microseconds):
    return pl.CostEstimate(
        flops=int(microseconds * 1e9), bytes_accessed=int(microseconds * 3e6), transcendentals=0
    )


def fence_kernel(token, out):
    out[0] = token[0]


def fence(token, *arrays):
    *arrays, token = lax.optimization_barrier((*arrays, token))
    scalar = pl.BlockSpec(memory_space=pltpu.SMEM)
    token = pl.pallas_call(
        fence_kernel,
        out_shape=jax.ShapeDtypeStruct((1,), jnp.int32),
        in_specs=[scalar],
        out_specs=scalar,
        cost_estimate=weight(50),
        name="fence",
    )(token)
    return (*arrays, token)


def attend_kernel(ids, live, q_ref, own_ref, low_ref, high_ref, out_ref, kv, sems):
    tiles = ids.shape[0]
    rows, width = q_ref.shape
    tile = rows // tiles
    heads = width // HEAD_DIM
    copies = [
        pltpu.make_async_copy(src, kv.at[:, pl.ds(i * rows, rows), :], sems.at[i])
        for i, src in enumerate((low_ref, own_ref, high_ref))
    ]
    for copy in copies:
        copy.start()
    for copy in copies:
        copy.wait()
    scale = math.log2(math.e) / math.sqrt(HEAD_DIM)
    key_row = lax.broadcasted_iota(jnp.int32, (KSEL * tile, 1), 0)
    lanes = [slice(h * HEAD_DIM, (h + 1) * HEAD_DIM) for h in range(heads)]

    def one_tile(t, carry):
        row = pl.multiple_of(t * tile, tile)
        starts = [pl.multiple_of(ids[t, s] * tile, tile) for s in range(KSEL)]

        def listed(which, lane):
            return jnp.concatenate([kv[which, pl.ds(s, tile), lane] for s in starts], axis=0)

        scores = jnp.concatenate(
            [
                lax.dot_general(
                    listed(0, lane),
                    q_ref[pl.ds(row, tile), lane],
                    (((1,), (1,)), ((), ())),
                    preferred_element_type=jnp.float32,
                )
                for lane in lanes
            ],
            axis=1,
        )
        scores = jnp.where(key_row < live[t] * tile, scores * scale, -1e30)
        expo = jnp.exp2(scores - jnp.max(scores, axis=0, keepdims=True))
        probs = (expo * (1.0 / jnp.sum(expo, axis=0, keepdims=True))).astype(jnp.bfloat16)
        for h, lane in enumerate(lanes):
            out_ref[pl.ds(row, tile), lane] = lax.dot_general(
                probs[:, h * tile : (h + 1) * tile],
                listed(1, lane),
                (((0,), (0,)), ((), ())),
                preferred_element_type=jnp.float32,
            ).astype(jnp.bfloat16)
        return carry

    lax.fori_loop(0, tiles, one_tile, 0)


def attend(queries, keyvals, low, high, pattern, live):
    rows, width = queries.shape
    tile_count = pattern.shape[0]
    local_ids = pattern - (lax.axis_index("frame") * tile_count - TILES_F)
    local_ids = jnp.clip(local_ids, 0, 3 * tile_count - 1)
    anywhere = pl.BlockSpec(memory_space=pl.ANY)
    scalars = pl.BlockSpec(memory_space=pltpu.SMEM)
    whole = pl.BlockSpec(memory_space=pltpu.VMEM)
    return pl.pallas_call(
        attend_kernel,
        out_shape=jax.ShapeDtypeStruct((rows, width), jnp.bfloat16),
        in_specs=[scalars, scalars, whole, anywhere, anywhere, anywhere],
        out_specs=whole,
        scratch_shapes=[
            pltpu.VMEM((2, 3 * rows, width), jnp.bfloat16),
            pltpu.SemaphoreType.DMA((3,)),
        ],
        compiler_params=pltpu.CompilerParams(vmem_limit_bytes=24 * MIB),
        cost_estimate=weight(8),
        name="attend",
    )(local_ids, live, queries, keyvals, low, high)


def halos(keyvals):
    count = lax.axis_size("frame")
    forward = [(i, i + 1) for i in range(count - 1)]
    backward = [(b, a) for a, b in forward]
    return lax.ppermute(keyvals, "frame", forward), lax.ppermute(keyvals, "frame", backward)


def plain(queries, keyvals, residual_in, gate, out_weight, pattern, live):
    low, high = halos(keyvals)
    attended = attend(queries, keyvals, low, high, pattern, live)
    weights = lax.all_gather(out_weight, "frame", axis=1, tiled=True)
    partial_rows = jnp.dot(attended, weights, preferred_element_type=jnp.float32)
    summed = lax.psum_scatter(
        partial_rows.astype(jnp.bfloat16), ("head", "sub"), scatter_dimension=1, tiled=True
    ).astype(jnp.float32)
    return residual_in + gate[None, :] * summed


def place(y, f, x, c):
    return ((y * 4 + f) * 2 + x) * 2 + c


def pairs(move, keep=lambda y, f, x, c: True):
    found = []
    for y in range(2):
        for f in range(4):
            for x in range(2):
                for c in range(2):
                    if keep(y, f, x, c):
                        found.append((place(y, f, x, c), place(*move(y, f, x, c))))
    return found


def block_at(k, f, x):
    return (f - k) % 4 if x == 0 else (f + k) % 4


def to_owner(steps, crosses):
    def move(y, f, x, c):
        g = block_at(steps[y ^ c][x], f, x)
        return c, f, g // 2, g % 2

    return pairs(move, lambda y, f, x, c: (y ^ c) in crosses)


def send(array, route, name):
    with jax.named_scope(name):
        return lax.ppermute(array, AXES, route)


def after(value, *earlier):
    return lax.optimization_barrier((value, *earlier))[0]


def finish_kernel(spot, *refs):
    residual, gate, out = refs[-3:]
    half = residual.shape[1] // 2
    count = (len(refs) - 3) // 2
    for cross, parts in ((0, refs[:count]), (1, refs[count : 2 * count])):
        lanes = pl.ds(pl.multiple_of((spot[0] ^ cross) * half, half), half)
        total = parts[0][...].astype(jnp.float32)
        for part in parts[1:]:
            total = total + part[...].astype(jnp.float32)
        out[:, lanes] = residual[:, lanes] + gate[:, lanes] * total


def finish(direct, crossed, residual_in, gate, spot):
    rows, width = residual_in.shape
    step = 128
    parts = [pl.BlockSpec((step, part.shape[1]), lambda i: (i, 0)) for part in direct + crossed]
    wide = pl.BlockSpec((step, width), lambda i: (i, 0))
    return pl.pallas_call(
        finish_kernel,
        grid=(rows // step,),
        out_shape=jax.ShapeDtypeStruct((rows, width), jnp.float32),
        in_specs=[pl.BlockSpec(memory_space=pltpu.SMEM)]
        + parts
        + [wide, pl.BlockSpec((1, width), lambda i: (0, 0))],
        out_specs=wide,
        compiler_params=pltpu.CompilerParams(vmem_limit_bytes=32 * MIB),
        name="finish",
    )(spot, *direct, *crossed, residual_in, gate[None, :])


def ringed(queries, keyvals, residual_in, gate, out_weight, pattern, live):
    y = lax.axis_index("groups")
    x = lax.axis_index("head")
    c = lax.axis_index("sub")
    half = out_weight.shape[1] // 2
    tie = lax.optimization_barrier

    ring = pairs(lambda y, f, x, c: (y, (f + 1) % 4 if x == 0 else (f - 1) % 4, x, c))
    sibling = pairs(lambda y, f, x, c: (y, f, x, 1 - c))
    here = y == c
    left = x == 0

    def to_owners(array, steps, name):
        return [
            send(array, to_owner((steps,) * 2, (0,)), "sums_" + name),
            send(array, to_owner((steps,) * 2, (1,)), "sums_cross_" + name),
        ]

    low, high = halos(keyvals)
    w0 = lax.dynamic_slice_in_dim(out_weight, y * half, half, axis=1)
    v0 = send(w0, sibling, "core_swap_0")
    w0, v0, low, high = tie((w0, v0, low, high))
    w1 = send(w0, ring, "ring_1")
    attended = attend(queries, keyvals, low, high, pattern, live)
    first = send(
        attended,
        pairs(lambda y, f, x, c: (1 - y, f, x, c) if c == y else (y, f, x, 1 - c)),
        "rows_1",
    )
    second = send(
        attended,
        pairs(lambda y, f, x, c: (1 - y, f, x, 1 - c), lambda y, f, x, c: c != y),
        "rows_2",
    )

    def region(token, body, *operands):
        shapes = jax.eval_shape(body, *operands)
        return lax.cond(
            token[0] > 0,
            body,
            lambda *_: jax.tree.map(lambda leaf: jnp.zeros(leaf.shape, leaf.dtype), shapes),
            *operands,
        )

    def sums(rows_own, rows_sib, own, sib):
        total = jnp.dot(rows_own, own, preferred_element_type=jnp.float32)
        total = total + jnp.dot(rows_sib, sib, preferred_element_type=jnp.float32)
        return total.astype(jnp.bfloat16)

    def swapped(w):
        return send(w, sibling, "core_swap")

    def begin(rows_own, rows_sib, w0, v0, w1):
        v1 = swapped(w1)
        s0 = sums(rows_own, rows_sib, w0, v0)
        return s0, sums(rows_own, rows_sib, w1, v1)

    def mix(rows_own, rows_sib, s0, w2):
        s2 = sums(rows_own, rows_sib, w2, swapped(w2))
        return jnp.where(left, s0, s2), jnp.where(left, s2, s0)

    def end(rows_own, rows_sib, w3):
        return sums(rows_own, rows_sib, w3, swapped(w3))

    w2 = send(w1, ring, "ring_2")
    w1, token = fence(live[:1], w1)
    first, second, token = tie((first, second, token))
    rows_own = jnp.where(here, attended, first)
    rows_sib = jnp.where(here, first, second)
    s0, s1 = region(token, begin, rows_own, rows_sib, w0, v0, w1)
    middle = to_owners(s1, (1, 1), "1")
    w2, s0 = tie((w2, s0))
    w3 = send(w2, ring, "ring_3")
    low_sum, high_sum = region(token, mix, rows_own, rows_sib, s0, w2)
    low_sum, high_sum, *middle = tie((low_sum, high_sum, *middle))
    early = to_owners(low_sum, (0, 2), "02") + to_owners(high_sum, (2, 0), "20")
    w3, low_sum, high_sum = tie((w3, low_sum, high_sum))
    s3 = region(token, end, rows_own, rows_sib, w3)
    middle += early
    last = to_owners(s3, (3, 3), "3")
    spot = jnp.reshape(y, (1,))
    base = finish(middle[::2], middle[1::2], residual_in, gate, spot)
    return finish(last[::2], last[1::2], base, gate, spot)


def solution(mesh):
    sizes = tuple(mesh.shape[axis] for axis in AXES)
    in_specs = (
        P(("groups", "frame"), ("head", "sub")),
        P(None, ("groups", "frame"), ("head", "sub")),
        P(("groups", "frame"), ("head", "sub")),
        P(("groups", "head", "sub")),
        P(("head", "sub"), "frame"),
        P(("groups", "frame"), None),
        P(("groups", "frame")),
    )
    return jax.shard_map(
        ringed if sizes == (2, 4, 2, 2) else plain,
        mesh=mesh,
        in_specs=in_specs,
        out_specs=P(("groups", "frame"), ("head", "sub")),
        check_vma=False,
    )
```

```python
import math

import jax
import jax.numpy as jnp
from jax import lax
from jax.experimental import pallas as pl
from jax.experimental.pallas import tpu as pltpu
from jax.sharding import PartitionSpec as P

HEAD_DIM = 128
TILES_F = 6
KSEL = 8
AXES = ("groups", "frame", "head", "sub")
MIB = 1 << 20


def weight(microseconds):
    return pl.CostEstimate(
        flops=int(microseconds * 1e9), bytes_accessed=int(microseconds * 3e6), transcendentals=0
    )


def fence_kernel(token, out):
    out[0] = token[0]


def fence(token, *arrays):
    *arrays, token = lax.optimization_barrier((*arrays, token))
    scalar = pl.BlockSpec(memory_space=pltpu.SMEM)
    token = pl.pallas_call(
        fence_kernel,
        out_shape=jax.ShapeDtypeStruct((1,), jnp.int32),
        in_specs=[scalar],
        out_specs=scalar,
        compiler_params=pltpu.CompilerParams(vmem_limit_bytes=MIB),
        cost_estimate=weight(50),
        name="fence",
    )(token)
    return (*arrays, token)


def attend_kernel(ids, live, q_ref, own_ref, low_ref, high_ref, out_ref, kv, sems):
    tiles = ids.shape[0]
    rows, width = q_ref.shape
    tile = rows // tiles
    heads = width // HEAD_DIM
    copies = [
        pltpu.make_async_copy(src, kv.at[:, pl.ds(i * rows, rows), :], sems.at[i])
        for i, src in enumerate((low_ref, own_ref, high_ref))
    ]
    for copy in copies:
        copy.start()
    for copy in copies:
        copy.wait()
    scale = math.log2(math.e) / math.sqrt(HEAD_DIM)
    key_row = lax.broadcasted_iota(jnp.int32, (KSEL * tile, 1), 0)
    lanes = [slice(h * HEAD_DIM, (h + 1) * HEAD_DIM) for h in range(heads)]

    def one_tile(t, carry):
        row = pl.multiple_of(t * tile, tile)
        starts = [pl.multiple_of(ids[t, s] * tile, tile) for s in range(KSEL)]

        def listed(which, lane):
            return jnp.concatenate([kv[which, pl.ds(s, tile), lane] for s in starts], axis=0)

        scores = jnp.concatenate(
            [
                lax.dot_general(
                    listed(0, lane),
                    q_ref[pl.ds(row, tile), lane],
                    (((1,), (1,)), ((), ())),
                    preferred_element_type=jnp.float32,
                )
                for lane in lanes
            ],
            axis=1,
        )
        scores = jnp.where(key_row < live[t] * tile, scores * scale, -1e30)
        expo = jnp.exp2(scores - jnp.max(scores, axis=0, keepdims=True))
        probs = (expo * (1.0 / jnp.sum(expo, axis=0, keepdims=True))).astype(jnp.bfloat16)
        for h, lane in enumerate(lanes):
            out_ref[pl.ds(row, tile), lane] = lax.dot_general(
                probs[:, h * tile : (h + 1) * tile],
                listed(1, lane),
                (((0,), (0,)), ((), ())),
                preferred_element_type=jnp.float32,
            ).astype(jnp.bfloat16)
        return carry

    lax.fori_loop(0, tiles, one_tile, 0)


def attend(queries, keyvals, low, high, pattern, live):
    rows, width = queries.shape
    tile_count = pattern.shape[0]
    local_ids = pattern - (lax.axis_index("frame") * tile_count - TILES_F)
    local_ids = jnp.clip(local_ids, 0, 3 * tile_count - 1)
    anywhere = pl.BlockSpec(memory_space=pl.ANY)
    scalars = pl.BlockSpec(memory_space=pltpu.SMEM)
    whole = pl.BlockSpec(memory_space=pltpu.VMEM)
    return pl.pallas_call(
        attend_kernel,
        out_shape=jax.ShapeDtypeStruct((rows, width), jnp.bfloat16),
        in_specs=[scalars, scalars, whole, anywhere, anywhere, anywhere],
        out_specs=whole,
        scratch_shapes=[
            pltpu.VMEM((2, 3 * rows, width), jnp.bfloat16),
            pltpu.SemaphoreType.DMA((3,)),
        ],
        compiler_params=pltpu.CompilerParams(vmem_limit_bytes=24 * MIB),
        cost_estimate=weight(8),
        name="attend",
    )(local_ids, live, queries, keyvals, low, high)


def halos(keyvals):
    count = lax.axis_size("frame")
    forward = [(i, i + 1) for i in range(count - 1)]
    backward = [(b, a) for a, b in forward]
    return lax.ppermute(keyvals, "frame", forward), lax.ppermute(keyvals, "frame", backward)


def plain(queries, keyvals, residual_in, gate, out_weight, pattern, live):
    low, high = halos(keyvals)
    attended = attend(queries, keyvals, low, high, pattern, live)
    weights = lax.all_gather(out_weight, "frame", axis=1, tiled=True)
    partial_rows = jnp.dot(attended, weights, preferred_element_type=jnp.float32)
    summed = lax.psum_scatter(
        partial_rows.astype(jnp.bfloat16), ("head", "sub"), scatter_dimension=1, tiled=True
    ).astype(jnp.float32)
    return residual_in + gate[None, :] * summed


def place(y, f, x, c):
    return ((y * 4 + f) * 2 + x) * 2 + c


def pairs(move, keep=lambda y, f, x, c: True):
    found = []
    for y in range(2):
        for f in range(4):
            for x in range(2):
                for c in range(2):
                    if keep(y, f, x, c):
                        found.append((place(y, f, x, c), place(*move(y, f, x, c))))
    return found


def block_at(k, f, x):
    return (f - k) % 4 if x == 0 else (f + k) % 4


def to_owner(steps, crosses):
    def move(y, f, x, c):
        g = block_at(steps[y ^ c][x], f, x)
        return c, f, g // 2, g % 2

    return pairs(move, lambda y, f, x, c: (y ^ c) in crosses)


def send(array, route, name):
    with jax.named_scope(name):
        return lax.ppermute(array, AXES, route)


def after(value, *earlier):
    return lax.optimization_barrier((value, *earlier))[0]


def finish_kernel(spot, *refs):
    residual, gate, out = refs[-3:]
    half = residual.shape[1] // 2
    count = (len(refs) - 3) // 2
    for cross, parts in ((0, refs[:count]), (1, refs[count : 2 * count])):
        lanes = pl.ds(pl.multiple_of((spot[0] ^ cross) * half, half), half)
        total = parts[0][...].astype(jnp.float32)
        for part in parts[1:]:
            total = total + part[...].astype(jnp.float32)
        out[:, lanes] = residual[:, lanes] + gate[:, lanes] * total


def finish(direct, crossed, residual_in, gate, spot):
    rows, width = residual_in.shape
    step = 128
    parts = [pl.BlockSpec((step, part.shape[1]), lambda i: (i, 0)) for part in direct + crossed]
    wide = pl.BlockSpec((step, width), lambda i: (i, 0))
    return pl.pallas_call(
        finish_kernel,
        grid=(rows // step,),
        out_shape=jax.ShapeDtypeStruct((rows, width), jnp.float32),
        in_specs=[pl.BlockSpec(memory_space=pltpu.SMEM)]
        + parts
        + [wide, pl.BlockSpec((1, width), lambda i: (0, 0))],
        out_specs=wide,
        compiler_params=pltpu.CompilerParams(vmem_limit_bytes=12 * MIB),
        name="finish",
    )(spot, *direct, *crossed, residual_in, gate[None, :])


def ringed(queries, keyvals, residual_in, gate, out_weight, pattern, live):
    y = lax.axis_index("groups")
    x = lax.axis_index("head")
    c = lax.axis_index("sub")
    half = out_weight.shape[1] // 2
    tie = lax.optimization_barrier

    ring = pairs(lambda y, f, x, c: (y, (f + 1) % 4 if x == 0 else (f - 1) % 4, x, c))
    sibling = pairs(lambda y, f, x, c: (y, f, x, 1 - c))
    here = y == c
    left = x == 0

    def to_owners(array, steps, name):
        return [
            send(array, to_owner((steps,) * 2, (0,)), "sums_" + name),
            send(array, to_owner((steps,) * 2, (1,)), "sums_cross_" + name),
        ]

    low, high = halos(keyvals)
    w0 = lax.dynamic_slice_in_dim(out_weight, y * half, half, axis=1)
    v0 = send(w0, sibling, "core_swap_0")
    w0, v0, low, high = tie((w0, v0, low, high))
    w1 = send(w0, ring, "ring_1")
    attended = attend(queries, keyvals, low, high, pattern, live)
    first = send(
        attended,
        pairs(lambda y, f, x, c: (1 - y, f, x, c) if c == y else (y, f, x, 1 - c)),
        "rows_1",
    )
    second = send(
        attended,
        pairs(lambda y, f, x, c: (1 - y, f, x, 1 - c), lambda y, f, x, c: c != y),
        "rows_2",
    )

    def region(token, body, *operands):
        shapes = jax.eval_shape(body, *operands)
        return lax.cond(
            token[0] > 0,
            body,
            lambda *_: jax.tree.map(lambda leaf: jnp.zeros(leaf.shape, leaf.dtype), shapes),
            *operands,
        )

    def sums(rows_own, rows_sib, own, sib):
        total = jnp.dot(rows_own, own, preferred_element_type=jnp.float32)
        total = total + jnp.dot(rows_sib, sib, preferred_element_type=jnp.float32)
        return total.astype(jnp.bfloat16)

    def swapped(w):
        return send(w, sibling, "core_swap")

    def begin(rows_own, rows_sib, w0, v0, w1):
        v1 = swapped(w1)
        s0 = sums(rows_own, rows_sib, w0, v0)
        return s0, sums(rows_own, rows_sib, w1, v1)

    def mix(rows_own, rows_sib, s0, w2):
        s2 = sums(rows_own, rows_sib, w2, swapped(w2))
        return jnp.where(left, s0, s2), jnp.where(left, s2, s0)

    def end(rows_own, rows_sib, w3):
        return sums(rows_own, rows_sib, w3, swapped(w3))

    w2 = send(w1, ring, "ring_2")
    w1, token = fence(live[:1], w1)
    first, second, token = tie((first, second, token))
    rows_own = jnp.where(here, attended, first)
    rows_sib = jnp.where(here, first, second)
    s0, s1 = region(token, begin, rows_own, rows_sib, w0, v0, w1)
    middle = to_owners(s1, (1, 1), "1")
    w2, s0 = tie((w2, s0))
    w3 = send(w2, ring, "ring_3")
    low_sum, high_sum = region(token, mix, rows_own, rows_sib, s0, w2)
    low_sum, high_sum, *middle = tie((low_sum, high_sum, *middle))
    early = to_owners(low_sum, (0, 2), "02") + to_owners(high_sum, (2, 0), "20")
    w3, low_sum, high_sum = tie((w3, low_sum, high_sum))
    s3 = region(token, end, rows_own, rows_sib, w3)
    middle += early
    last = to_owners(s3, (3, 3), "3")
    spot = jnp.reshape(y, (1,))
    base = finish(middle[::2], middle[1::2], residual_in, gate, spot)
    return finish(last[::2], last[1::2], base, gate, spot)


def solution(mesh):
    sizes = tuple(mesh.shape[axis] for axis in AXES)
    in_specs = (
        P(("groups", "frame"), ("head", "sub")),
        P(None, ("groups", "frame"), ("head", "sub")),
        P(("groups", "frame"), ("head", "sub")),
        P(("groups", "head", "sub")),
        P(("head", "sub"), "frame"),
        P(("groups", "frame"), None),
        P(("groups", "frame")),
    )
    return jax.shard_map(
        ringed if sizes == (2, 4, 2, 2) else plain,
        mesh=mesh,
        in_specs=in_specs,
        out_specs=P(("groups", "frame"), ("head", "sub")),
        check_vma=False,
    )
```

```python
import math

import jax
import jax.numpy as jnp
from jax import lax
from jax.experimental import pallas as pl
from jax.experimental.pallas import tpu as pltpu
from jax.sharding import PartitionSpec as P

HEAD_DIM = 128
TILES_F = 6
KSEL = 8
AXES = ("groups", "frame", "head", "sub")
MIB = 1 << 20


def weight(microseconds):
    return pl.CostEstimate(
        flops=int(microseconds * 1e9), bytes_accessed=int(microseconds * 3e6), transcendentals=0
    )


def fence_kernel(token, out):
    out[0] = token[0]


def fence(token, *arrays):
    *arrays, token = lax.optimization_barrier((*arrays, token))
    scalar = pl.BlockSpec(memory_space=pltpu.SMEM)
    token = pl.pallas_call(
        fence_kernel,
        out_shape=jax.ShapeDtypeStruct((1,), jnp.int32),
        in_specs=[scalar],
        out_specs=scalar,
        compiler_params=pltpu.CompilerParams(vmem_limit_bytes=MIB),
        cost_estimate=weight(50),
        name="fence",
    )(token)
    return (*arrays, token)


def attend_kernel(ids, live, q_ref, own_ref, low_ref, high_ref, out_ref, kv, sems):
    tiles = ids.shape[0]
    rows, width = q_ref.shape
    tile = rows // tiles
    heads = width // HEAD_DIM
    copies = [
        pltpu.make_async_copy(src, kv.at[:, pl.ds(i * rows, rows), :], sems.at[i])
        for i, src in enumerate((low_ref, own_ref, high_ref))
    ]
    for copy in copies:
        copy.start()
    for copy in copies:
        copy.wait()
    scale = math.log2(math.e) / math.sqrt(HEAD_DIM)
    key_row = lax.broadcasted_iota(jnp.int32, (KSEL * tile, 1), 0)
    lanes = [slice(h * HEAD_DIM, (h + 1) * HEAD_DIM) for h in range(heads)]

    def one_tile(t, carry):
        row = pl.multiple_of(t * tile, tile)
        starts = [pl.multiple_of(ids[t, s] * tile, tile) for s in range(KSEL)]

        def listed(which, lane):
            return jnp.concatenate([kv[which, pl.ds(s, tile), lane] for s in starts], axis=0)

        scores = jnp.concatenate(
            [
                lax.dot_general(
                    listed(0, lane),
                    q_ref[pl.ds(row, tile), lane],
                    (((1,), (1,)), ((), ())),
                    preferred_element_type=jnp.float32,
                )
                for lane in lanes
            ],
            axis=1,
        )
        scores = jnp.where(key_row < live[t] * tile, scores * scale, -1e30)
        expo = jnp.exp2(scores - jnp.max(scores, axis=0, keepdims=True))
        probs = (expo * (1.0 / jnp.sum(expo, axis=0, keepdims=True))).astype(jnp.bfloat16)
        for h, lane in enumerate(lanes):
            out_ref[pl.ds(row, tile), lane] = lax.dot_general(
                probs[:, h * tile : (h + 1) * tile],
                listed(1, lane),
                (((0,), (0,)), ((), ())),
                preferred_element_type=jnp.float32,
            ).astype(jnp.bfloat16)
        return carry

    lax.fori_loop(0, tiles, one_tile, 0)


def attend(queries, keyvals, low, high, pattern, live):
    rows, width = queries.shape
    tile_count = pattern.shape[0]
    local_ids = pattern - (lax.axis_index("frame") * tile_count - TILES_F)
    local_ids = jnp.clip(local_ids, 0, 3 * tile_count - 1)
    anywhere = pl.BlockSpec(memory_space=pl.ANY)
    scalars = pl.BlockSpec(memory_space=pltpu.SMEM)
    whole = pl.BlockSpec(memory_space=pltpu.VMEM)
    return pl.pallas_call(
        attend_kernel,
        out_shape=jax.ShapeDtypeStruct((rows, width), jnp.bfloat16),
        in_specs=[scalars, scalars, whole, anywhere, anywhere, anywhere],
        out_specs=whole,
        scratch_shapes=[
            pltpu.VMEM((2, 3 * rows, width), jnp.bfloat16),
            pltpu.SemaphoreType.DMA((3,)),
        ],
        compiler_params=pltpu.CompilerParams(vmem_limit_bytes=24 * MIB),
        cost_estimate=weight(8),
        name="attend",
    )(local_ids, live, queries, keyvals, low, high)


def halos(keyvals):
    count = lax.axis_size("frame")
    forward = [(i, i + 1) for i in range(count - 1)]
    backward = [(b, a) for a, b in forward]
    return lax.ppermute(keyvals, "frame", forward), lax.ppermute(keyvals, "frame", backward)


def plain(queries, keyvals, residual_in, gate, out_weight, pattern, live):
    low, high = halos(keyvals)
    attended = attend(queries, keyvals, low, high, pattern, live)
    weights = lax.all_gather(out_weight, "frame", axis=1, tiled=True)
    partial_rows = jnp.dot(attended, weights, preferred_element_type=jnp.float32)
    summed = lax.psum_scatter(
        partial_rows.astype(jnp.bfloat16), ("head", "sub"), scatter_dimension=1, tiled=True
    ).astype(jnp.float32)
    return residual_in + gate[None, :] * summed


def place(y, f, x, c):
    return ((y * 4 + f) * 2 + x) * 2 + c


def pairs(move, keep=lambda y, f, x, c: True):
    found = []
    for y in range(2):
        for f in range(4):
            for x in range(2):
                for c in range(2):
                    if keep(y, f, x, c):
                        found.append((place(y, f, x, c), place(*move(y, f, x, c))))
    return found


def block_at(k, f, x):
    return (f - k) % 4 if x == 0 else (f + k) % 4


def to_owner(steps, crosses):
    def move(y, f, x, c):
        g = block_at(steps[y ^ c][x], f, x)
        return c, f, g // 2, g % 2

    return pairs(move, lambda y, f, x, c: (y ^ c) in crosses)


def send(array, route, name):
    with jax.named_scope(name):
        return lax.ppermute(array, AXES, route)


def after(value, *earlier):
    return lax.optimization_barrier((value, *earlier))[0]


def finish_kernel(spot, *refs):
    residual, gate, out = refs[-3:]
    half = residual.shape[1] // 2
    count = (len(refs) - 3) // 2
    for cross, parts in ((0, refs[:count]), (1, refs[count : 2 * count])):
        lanes = pl.ds(pl.multiple_of((spot[0] ^ cross) * half, half), half)
        total = parts[0][...].astype(jnp.float32)
        for part in parts[1:]:
            total = total + part[...].astype(jnp.float32)
        out[:, lanes] = residual[:, lanes] + gate[:, lanes] * total


def finish(direct, crossed, residual_in, gate, spot):
    rows, width = residual_in.shape
    step = rows // 2
    parts = [pl.BlockSpec((step, part.shape[1]), lambda i: (i, 0)) for part in direct + crossed]
    wide = pl.BlockSpec((step, width), lambda i: (i, 0))
    return pl.pallas_call(
        finish_kernel,
        grid=(rows // step,),
        out_shape=jax.ShapeDtypeStruct((rows, width), jnp.float32),
        in_specs=[pl.BlockSpec(memory_space=pltpu.SMEM)]
        + parts
        + [wide, pl.BlockSpec((1, width), lambda i: (0, 0))],
        out_specs=wide,
        compiler_params=pltpu.CompilerParams(vmem_limit_bytes=24 * MIB),
        name="finish",
    )(spot, *direct, *crossed, residual_in, gate[None, :])


def ringed(queries, keyvals, residual_in, gate, out_weight, pattern, live):
    y = lax.axis_index("groups")
    x = lax.axis_index("head")
    c = lax.axis_index("sub")
    half = out_weight.shape[1] // 2
    tie = lax.optimization_barrier

    ring = pairs(lambda y, f, x, c: (y, (f + 1) % 4 if x == 0 else (f - 1) % 4, x, c))
    sibling = pairs(lambda y, f, x, c: (y, f, x, 1 - c))
    here = y == c
    left = x == 0

    def to_owners(array, steps, name):
        return [
            send(array, to_owner((steps,) * 2, (0,)), "sums_" + name),
            send(array, to_owner((steps,) * 2, (1,)), "sums_cross_" + name),
        ]

    low, high = halos(keyvals)
    w0 = lax.dynamic_slice_in_dim(out_weight, y * half, half, axis=1)
    v0 = send(w0, sibling, "core_swap_0")
    w0, low = tie((w0, low))
    w1 = send(w0, ring, "ring_1")
    attended = attend(queries, keyvals, low, high, pattern, live)
    first = send(
        attended,
        pairs(lambda y, f, x, c: (1 - y, f, x, c) if c == y else (y, f, x, 1 - c)),
        "rows_1",
    )
    second = send(
        attended,
        pairs(lambda y, f, x, c: (1 - y, f, x, 1 - c), lambda y, f, x, c: c != y),
        "rows_2",
    )

    def region(token, body, *operands):
        shapes = jax.eval_shape(body, *operands)
        return lax.cond(
            token[0] > 0,
            body,
            lambda *_: jax.tree.map(lambda leaf: jnp.zeros(leaf.shape, leaf.dtype), shapes),
            *operands,
        )

    def sums(rows_own, rows_sib, own, sib):
        total = jnp.dot(rows_own, own, preferred_element_type=jnp.float32)
        total = total + jnp.dot(rows_sib, sib, preferred_element_type=jnp.float32)
        return total.astype(jnp.bfloat16)

    def swapped(w):
        return send(w, sibling, "core_swap")

    def begin(rows_own, rows_sib, w1):
        return sums(rows_own, rows_sib, w1, swapped(w1))

    def mix(rows_own, rows_sib, s0, w2):
        s2 = sums(rows_own, rows_sib, w2, swapped(w2))
        return jnp.where(left, s0, s2), jnp.where(left, s2, s0)

    def end(rows_own, rows_sib, w3):
        return sums(rows_own, rows_sib, w3, swapped(w3))

    w2 = send(w1, ring, "ring_2")
    w1, token = fence(live[:1], w1)
    first, second, token = tie((first, second, token))
    rows_own = jnp.where(here, attended, first)
    rows_sib = jnp.where(here, first, second)
    s1 = region(token, begin, rows_own, rows_sib, w1)
    middle = to_owners(s1, (1, 1), "1")
    s0 = region(token, sums, rows_own, rows_sib, w0, v0)
    w2, s0 = tie((w2, s0))
    w3 = send(w2, ring, "ring_3")
    low_sum, high_sum = region(token, mix, rows_own, rows_sib, s0, w2)
    low_sum, high_sum, *middle = tie((low_sum, high_sum, *middle))
    early = to_owners(low_sum, (0, 2), "02") + to_owners(high_sum, (2, 0), "20")
    w3, low_sum, high_sum = tie((w3, low_sum, high_sum))
    s3 = region(token, end, rows_own, rows_sib, w3)
    middle += early
    last = to_owners(s3, (3, 3), "3")
    spot = jnp.reshape(y, (1,))
    base = finish(middle[::2], middle[1::2], residual_in, gate, spot)
    return finish(last[::2], last[1::2], base, gate, spot)


def solution(mesh):
    sizes = tuple(mesh.shape[axis] for axis in AXES)
    in_specs = (
        P(("groups", "frame"), ("head", "sub")),
        P(None, ("groups", "frame"), ("head", "sub")),
        P(("groups", "frame"), ("head", "sub")),
        P(("groups", "head", "sub")),
        P(("head", "sub"), "frame"),
        P(("groups", "frame"), None),
        P(("groups", "frame")),
    )
    return jax.shard_map(
        ringed if sizes == (2, 4, 2, 2) else plain,
        mesh=mesh,
        in_specs=in_specs,
        out_specs=P(("groups", "frame"), ("head", "sub")),
        check_vma=False,
    )
```

```python
import math

import jax
import jax.numpy as jnp
from jax import lax
from jax.experimental import pallas as pl
from jax.experimental.pallas import tpu as pltpu
from jax.sharding import PartitionSpec as P

HEAD_DIM = 128
TILES_F = 6
KSEL = 8
AXES = ("groups", "frame", "head", "sub")
MIB = 1 << 20


def weight(microseconds):
    return pl.CostEstimate(
        flops=int(microseconds * 1e9), bytes_accessed=int(microseconds * 3e6), transcendentals=0
    )


def fence_kernel(token, out):
    out[0] = token[0]


def fence(token, *arrays):
    *arrays, token = lax.optimization_barrier((*arrays, token))
    scalar = pl.BlockSpec(memory_space=pltpu.SMEM)
    token = pl.pallas_call(
        fence_kernel,
        out_shape=jax.ShapeDtypeStruct((1,), jnp.int32),
        in_specs=[scalar],
        out_specs=scalar,
        compiler_params=pltpu.CompilerParams(vmem_limit_bytes=MIB),
        cost_estimate=weight(50),
        name="fence",
    )(token)
    return (*arrays, token)


def attend_kernel(ids, live, q_ref, own_ref, low_ref, high_ref, out_ref, kv, sems):
    tiles = ids.shape[0]
    rows, width = q_ref.shape
    tile = rows // tiles
    heads = width // HEAD_DIM
    copies = [
        pltpu.make_async_copy(src, kv.at[:, pl.ds(i * rows, rows), :], sems.at[i])
        for i, src in enumerate((low_ref, own_ref, high_ref))
    ]
    for copy in copies:
        copy.start()
    for copy in copies:
        copy.wait()
    scale = math.log2(math.e) / math.sqrt(HEAD_DIM)
    key_row = lax.broadcasted_iota(jnp.int32, (KSEL * tile, 1), 0)
    lanes = [slice(h * HEAD_DIM, (h + 1) * HEAD_DIM) for h in range(heads)]

    def one_tile(t, carry):
        row = pl.multiple_of(t * tile, tile)
        starts = [pl.multiple_of(ids[t, s] * tile, tile) for s in range(KSEL)]

        def listed(which, lane):
            return jnp.concatenate([kv[which, pl.ds(s, tile), lane] for s in starts], axis=0)

        scores = jnp.concatenate(
            [
                lax.dot_general(
                    listed(0, lane),
                    q_ref[pl.ds(row, tile), lane],
                    (((1,), (1,)), ((), ())),
                    preferred_element_type=jnp.float32,
                )
                for lane in lanes
            ],
            axis=1,
        )
        scores = jnp.where(key_row < live[t] * tile, scores * scale, -1e30)
        expo = jnp.exp2(scores - jnp.max(scores, axis=0, keepdims=True))
        probs = (expo * (1.0 / jnp.sum(expo, axis=0, keepdims=True))).astype(jnp.bfloat16)
        for h, lane in enumerate(lanes):
            out_ref[pl.ds(row, tile), lane] = lax.dot_general(
                probs[:, h * tile : (h + 1) * tile],
                listed(1, lane),
                (((0,), (0,)), ((), ())),
                preferred_element_type=jnp.float32,
            ).astype(jnp.bfloat16)
        return carry

    lax.fori_loop(0, tiles, one_tile, 0)


def attend(queries, keyvals, low, high, pattern, live):
    rows, width = queries.shape
    tile_count = pattern.shape[0]
    local_ids = pattern - (lax.axis_index("frame") * tile_count - TILES_F)
    local_ids = jnp.clip(local_ids, 0, 3 * tile_count - 1)
    anywhere = pl.BlockSpec(memory_space=pl.ANY)
    scalars = pl.BlockSpec(memory_space=pltpu.SMEM)
    whole = pl.BlockSpec(memory_space=pltpu.VMEM)
    return pl.pallas_call(
        attend_kernel,
        out_shape=jax.ShapeDtypeStruct((rows, width), jnp.bfloat16),
        in_specs=[scalars, scalars, whole, anywhere, anywhere, anywhere],
        out_specs=whole,
        scratch_shapes=[
            pltpu.VMEM((2, 3 * rows, width), jnp.bfloat16),
            pltpu.SemaphoreType.DMA((3,)),
        ],
        compiler_params=pltpu.CompilerParams(vmem_limit_bytes=24 * MIB),
        cost_estimate=weight(8),
        name="attend",
    )(local_ids, live, queries, keyvals, low, high)


def halos(keyvals):
    count = lax.axis_size("frame")
    forward = [(i, i + 1) for i in range(count - 1)]
    backward = [(b, a) for a, b in forward]
    return lax.ppermute(keyvals, "frame", forward), lax.ppermute(keyvals, "frame", backward)


def plain(queries, keyvals, residual_in, gate, out_weight, pattern, live):
    low, high = halos(keyvals)
    attended = attend(queries, keyvals, low, high, pattern, live)
    weights = lax.all_gather(out_weight, "frame", axis=1, tiled=True)
    partial_rows = jnp.dot(attended, weights, preferred_element_type=jnp.float32)
    summed = lax.psum_scatter(
        partial_rows.astype(jnp.bfloat16), ("head", "sub"), scatter_dimension=1, tiled=True
    ).astype(jnp.float32)
    return residual_in + gate[None, :] * summed


def place(y, f, x, c):
    return ((y * 4 + f) * 2 + x) * 2 + c


def pairs(move, keep=lambda y, f, x, c: True):
    found = []
    for y in range(2):
        for f in range(4):
            for x in range(2):
                for c in range(2):
                    if keep(y, f, x, c):
                        found.append((place(y, f, x, c), place(*move(y, f, x, c))))
    return found


def block_at(k, f, x):
    return (f - k) % 4 if x == 0 else (f + k) % 4


def to_owner(steps, crosses):
    def move(y, f, x, c):
        g = block_at(steps[y ^ c][x], f, x)
        return c, f, g // 2, g % 2

    return pairs(move, lambda y, f, x, c: (y ^ c) in crosses)


def send(array, route, name):
    with jax.named_scope(name):
        return lax.ppermute(array, AXES, route)


def after(value, *earlier):
    return lax.optimization_barrier((value, *earlier))[0]


def finish_kernel(spot, *refs):
    residual, gate, out = refs[-3:]
    half = residual.shape[1] // 2
    count = (len(refs) - 3) // 2
    for cross, parts in ((0, refs[:count]), (1, refs[count : 2 * count])):
        lanes = pl.ds(pl.multiple_of((spot[0] ^ cross) * half, half), half)
        total = parts[0][...].astype(jnp.float32)
        for part in parts[1:]:
            total = total + part[...].astype(jnp.float32)
        out[:, lanes] = residual[:, lanes] + gate[:, lanes] * total


def finish(direct, crossed, residual_in, gate, spot):
    rows, width = residual_in.shape
    step = rows // 2
    parts = [pl.BlockSpec((step, part.shape[1]), lambda i: (i, 0)) for part in direct + crossed]
    wide = pl.BlockSpec((step, width), lambda i: (i, 0))
    return pl.pallas_call(
        finish_kernel,
        grid=(rows // step,),
        out_shape=jax.ShapeDtypeStruct((rows, width), jnp.float32),
        in_specs=[pl.BlockSpec(memory_space=pltpu.SMEM)]
        + parts
        + [wide, pl.BlockSpec((1, width), lambda i: (0, 0))],
        out_specs=wide,
        compiler_params=pltpu.CompilerParams(vmem_limit_bytes=24 * MIB),
        name="finish",
    )(spot, *direct, *crossed, residual_in, gate[None, :])


def ringed(queries, keyvals, residual_in, gate, out_weight, pattern, live):
    y = lax.axis_index("groups")
    x = lax.axis_index("head")
    c = lax.axis_index("sub")
    half = out_weight.shape[1] // 2
    tie = lax.optimization_barrier

    ring = pairs(lambda y, f, x, c: (y, (f + 1) % 4 if x == 0 else (f - 1) % 4, x, c))
    back = [(target, source) for source, target in ring]
    sibling = pairs(lambda y, f, x, c: (y, f, x, 1 - c))
    here = y == c
    left = x == 0

    def to_owners(array, steps, name):
        return [
            send(array, to_owner((steps,) * 2, (0,)), "sums_" + name),
            send(array, to_owner((steps,) * 2, (1,)), "sums_cross_" + name),
        ]

    low, high = halos(keyvals)
    w0 = lax.dynamic_slice_in_dim(out_weight, y * half, half, axis=1)
    v0 = send(w0, sibling, "core_swap_0")
    w0, low = tie((w0, low))
    w1 = send(w0, ring, "ring_1")
    attended = attend(queries, keyvals, low, high, pattern, live)
    first = send(
        attended,
        pairs(lambda y, f, x, c: (1 - y, f, x, c) if c == y else (y, f, x, 1 - c)),
        "rows_1",
    )
    second = send(
        attended,
        pairs(lambda y, f, x, c: (1 - y, f, x, 1 - c), lambda y, f, x, c: c != y),
        "rows_2",
    )

    def region(token, body, *operands):
        shapes = jax.eval_shape(body, *operands)
        return lax.cond(
            token[0] > 0,
            body,
            lambda *_: jax.tree.map(lambda leaf: jnp.zeros(leaf.shape, leaf.dtype), shapes),
            *operands,
        )

    def sums(rows_own, rows_sib, own, sib):
        total = jnp.dot(rows_own, own, preferred_element_type=jnp.float32)
        total = total + jnp.dot(rows_sib, sib, preferred_element_type=jnp.float32)
        return total.astype(jnp.bfloat16)

    def swapped(w):
        return send(w, sibling, "core_swap")

    def begin(rows_own, rows_sib, w1):
        return sums(rows_own, rows_sib, w1, swapped(w1))

    def mix(rows_own, rows_sib, s0, w2):
        s2 = sums(rows_own, rows_sib, w2, swapped(w2))
        return jnp.where(left, s0, s2), jnp.where(left, s2, s0)

    def end(rows_own, rows_sib, w3):
        return sums(rows_own, rows_sib, w3, swapped(w3))

    w2 = send(w1, ring, "ring_2")
    w1, token = fence(live[:1], w1)
    first, second, token = tie((first, second, token))
    rows_own = jnp.where(here, attended, first)
    rows_sib = jnp.where(here, first, second)
    s1 = region(token, begin, rows_own, rows_sib, w1)
    middle = to_owners(s1, (1, 1), "1")
    s0 = region(token, sums, rows_own, rows_sib, w0, v0)
    w2, s0 = tie((w2, s0))
    w3 = send(w0, back, "ring_after")
    low_sum, high_sum = region(token, mix, rows_own, rows_sib, s0, w2)
    low_sum, high_sum, *middle = tie((low_sum, high_sum, *middle))
    early = to_owners(low_sum, (0, 2), "02") + to_owners(high_sum, (2, 0), "20")
    w3, low_sum, high_sum = tie((w3, low_sum, high_sum))
    s3 = region(token, end, rows_own, rows_sib, w3)
    middle += early
    last = to_owners(s3, (3, 3), "3")
    spot = jnp.reshape(y, (1,))
    base = finish(middle[::2], middle[1::2], residual_in, gate, spot)
    return finish(last[::2], last[1::2], base, gate, spot)


def solution(mesh):
    sizes = tuple(mesh.shape[axis] for axis in AXES)
    in_specs = (
        P(("groups", "frame"), ("head", "sub")),
        P(None, ("groups", "frame"), ("head", "sub")),
        P(("groups", "frame"), ("head", "sub")),
        P(("groups", "head", "sub")),
        P(("head", "sub"), "frame"),
        P(("groups", "frame"), None),
        P(("groups", "frame")),
    )
    return jax.shard_map(
        ringed if sizes == (2, 4, 2, 2) else plain,
        mesh=mesh,
        in_specs=in_specs,
        out_specs=P(("groups", "frame"), ("head", "sub")),
        check_vma=False,
    )
```

```python
import math

import jax
import jax.numpy as jnp
from jax import lax
from jax.experimental import pallas as pl
from jax.experimental.pallas import tpu as pltpu
from jax.sharding import PartitionSpec as P

HEAD_DIM = 128
TILES_F = 6
KSEL = 8
AXES = ("groups", "frame", "head", "sub")
MIB = 1 << 20


def weight(microseconds):
    return pl.CostEstimate(
        flops=int(microseconds * 1e9), bytes_accessed=int(microseconds * 3e6), transcendentals=0
    )


def fence_kernel(token, out):
    out[0] = token[0]


def fence(token, *arrays):
    *arrays, token = lax.optimization_barrier((*arrays, token))
    scalar = pl.BlockSpec(memory_space=pltpu.SMEM)
    token = pl.pallas_call(
        fence_kernel,
        out_shape=jax.ShapeDtypeStruct((1,), jnp.int32),
        in_specs=[scalar],
        out_specs=scalar,
        compiler_params=pltpu.CompilerParams(vmem_limit_bytes=MIB),
        cost_estimate=weight(50),
        name="fence",
    )(token)
    return (*arrays, token)


def attend_kernel(ids, live, q_ref, own_ref, low_ref, high_ref, out_ref, kv, sems):
    tiles = ids.shape[0]
    rows, width = q_ref.shape
    tile = rows // tiles
    heads = width // HEAD_DIM
    copies = [
        pltpu.make_async_copy(src, kv.at[:, pl.ds(i * rows, rows), :], sems.at[i])
        for i, src in enumerate((low_ref, own_ref, high_ref))
    ]
    for copy in copies:
        copy.start()
    for copy in copies:
        copy.wait()
    scale = math.log2(math.e) / math.sqrt(HEAD_DIM)
    key_row = lax.broadcasted_iota(jnp.int32, (KSEL * tile, 1), 0)
    lanes = [slice(h * HEAD_DIM, (h + 1) * HEAD_DIM) for h in range(heads)]

    def one_tile(t, carry):
        row = pl.multiple_of(t * tile, tile)
        starts = [pl.multiple_of(ids[t, s] * tile, tile) for s in range(KSEL)]

        def listed(which, lane):
            return jnp.concatenate([kv[which, pl.ds(s, tile), lane] for s in starts], axis=0)

        scores = jnp.concatenate(
            [
                lax.dot_general(
                    listed(0, lane),
                    q_ref[pl.ds(row, tile), lane],
                    (((1,), (1,)), ((), ())),
                    preferred_element_type=jnp.float32,
                )
                for lane in lanes
            ],
            axis=1,
        )
        scores = jnp.where(key_row < live[t] * tile, scores * scale, -1e30)
        expo = jnp.exp2(scores - jnp.max(scores, axis=0, keepdims=True))
        probs = (expo * (1.0 / jnp.sum(expo, axis=0, keepdims=True))).astype(jnp.bfloat16)
        for h, lane in enumerate(lanes):
            out_ref[pl.ds(row, tile), lane] = lax.dot_general(
                probs[:, h * tile : (h + 1) * tile],
                listed(1, lane),
                (((0,), (0,)), ((), ())),
                preferred_element_type=jnp.float32,
            ).astype(jnp.bfloat16)
        return carry

    lax.fori_loop(0, tiles, one_tile, 0)


def attend(queries, keyvals, low, high, pattern, live):
    rows, width = queries.shape
    tile_count = pattern.shape[0]
    local_ids = pattern - (lax.axis_index("frame") * tile_count - TILES_F)
    local_ids = jnp.clip(local_ids, 0, 3 * tile_count - 1)
    anywhere = pl.BlockSpec(memory_space=pl.ANY)
    scalars = pl.BlockSpec(memory_space=pltpu.SMEM)
    whole = pl.BlockSpec(memory_space=pltpu.VMEM)
    return pl.pallas_call(
        attend_kernel,
        out_shape=jax.ShapeDtypeStruct((rows, width), jnp.bfloat16),
        in_specs=[scalars, scalars, whole, anywhere, anywhere, anywhere],
        out_specs=whole,
        scratch_shapes=[
            pltpu.VMEM((2, 3 * rows, width), jnp.bfloat16),
            pltpu.SemaphoreType.DMA((3,)),
        ],
        compiler_params=pltpu.CompilerParams(vmem_limit_bytes=24 * MIB),
        cost_estimate=weight(8),
        name="attend",
    )(local_ids, live, queries, keyvals, low, high)


def halos(keyvals):
    count = lax.axis_size("frame")
    forward = [(i, i + 1) for i in range(count - 1)]
    backward = [(b, a) for a, b in forward]
    return lax.ppermute(keyvals, "frame", forward), lax.ppermute(keyvals, "frame", backward)


def plain(queries, keyvals, residual_in, gate, out_weight, pattern, live):
    low, high = halos(keyvals)
    attended = attend(queries, keyvals, low, high, pattern, live)
    weights = lax.all_gather(out_weight, "frame", axis=1, tiled=True)
    partial_rows = jnp.dot(attended, weights, preferred_element_type=jnp.float32)
    summed = lax.psum_scatter(
        partial_rows.astype(jnp.bfloat16), ("head", "sub"), scatter_dimension=1, tiled=True
    ).astype(jnp.float32)
    return residual_in + gate[None, :] * summed


def place(y, f, x, c):
    return ((y * 4 + f) * 2 + x) * 2 + c


def pairs(move, keep=lambda y, f, x, c: True):
    found = []
    for y in range(2):
        for f in range(4):
            for x in range(2):
                for c in range(2):
                    if keep(y, f, x, c):
                        found.append((place(y, f, x, c), place(*move(y, f, x, c))))
    return found


def block_at(k, f, x):
    return (f - k) % 4 if x == 0 else (f + k) % 4


def to_owner(steps, crosses):
    def move(y, f, x, c):
        g = block_at(steps[y ^ c][x], f, x)
        return c, f, g // 2, g % 2

    return pairs(move, lambda y, f, x, c: (y ^ c) in crosses)


def send(array, route, name):
    with jax.named_scope(name):
        return lax.ppermute(array, AXES, route)


def after(value, *earlier):
    return lax.optimization_barrier((value, *earlier))[0]


def finish_kernel(spot, *refs):
    residual, gate, out = refs[-3:]
    half = residual.shape[1] // 2
    count = (len(refs) - 3) // 2
    for cross, parts in ((0, refs[:count]), (1, refs[count : 2 * count])):
        lanes = pl.ds(pl.multiple_of((spot[0] ^ cross) * half, half), half)
        total = parts[0][...].astype(jnp.float32)
        for part in parts[1:]:
            total = total + part[...].astype(jnp.float32)
        out[:, lanes] = residual[:, lanes] + gate[:, lanes] * total


def finish(direct, crossed, residual_in, gate, spot):
    rows, width = residual_in.shape
    step = rows // 2
    parts = [pl.BlockSpec((step, part.shape[1]), lambda i: (i, 0)) for part in direct + crossed]
    wide = pl.BlockSpec((step, width), lambda i: (i, 0))
    return pl.pallas_call(
        finish_kernel,
        grid=(rows // step,),
        out_shape=jax.ShapeDtypeStruct((rows, width), jnp.float32),
        in_specs=[pl.BlockSpec(memory_space=pltpu.SMEM)]
        + parts
        + [wide, pl.BlockSpec((1, width), lambda i: (0, 0))],
        out_specs=wide,
        compiler_params=pltpu.CompilerParams(vmem_limit_bytes=24 * MIB),
        name="finish",
    )(spot, *direct, *crossed, residual_in, gate[None, :])


def ringed(queries, keyvals, residual_in, gate, out_weight, pattern, live):
    y = lax.axis_index("groups")
    x = lax.axis_index("head")
    c = lax.axis_index("sub")
    half = out_weight.shape[1] // 2
    tie = lax.optimization_barrier

    ring = pairs(lambda y, f, x, c: (y, (f + 1) % 4 if x == 0 else (f - 1) % 4, x, c))
    back = [(target, source) for source, target in ring]
    sibling = pairs(lambda y, f, x, c: (y, f, x, 1 - c))
    here = y == c
    left = x == 0

    def to_owners(array, steps, name):
        return [
            send(array, to_owner((steps,) * 2, (0,)), "sums_" + name),
            send(array, to_owner((steps,) * 2, (1,)), "sums_cross_" + name),
        ]

    low, high = halos(keyvals)
    w0 = lax.dynamic_slice_in_dim(out_weight, y * half, half, axis=1)
    v0 = send(w0, sibling, "core_swap_0")
    w0, low = tie((w0, low))
    w1 = send(w0, ring, "ring_1")
    attended = attend(queries, keyvals, low, high, pattern, live)
    first = send(
        attended,
        pairs(lambda y, f, x, c: (1 - y, f, x, c) if c == y else (y, f, x, 1 - c)),
        "rows_1",
    )
    second = send(
        attended,
        pairs(lambda y, f, x, c: (1 - y, f, x, 1 - c), lambda y, f, x, c: c != y),
        "rows_2",
    )

    def region(token, body, *operands):
        shapes = jax.eval_shape(body, *operands)
        return lax.cond(
            token[0] > 0,
            body,
            lambda *_: jax.tree.map(lambda leaf: jnp.zeros(leaf.shape, leaf.dtype), shapes),
            *operands,
        )

    def sums(rows_own, rows_sib, own, sib):
        total = jnp.dot(rows_own, own, preferred_element_type=jnp.float32)
        total = total + jnp.dot(rows_sib, sib, preferred_element_type=jnp.float32)
        return total.astype(jnp.bfloat16)

    def swapped(w):
        return send(w, sibling, "core_swap")

    def begin(rows_own, rows_sib, w1):
        return sums(rows_own, rows_sib, w1, swapped(w1))

    def mix(rows_own, rows_sib, w0, v0, w2):
        v2 = swapped(w2)
        s0 = sums(rows_own, rows_sib, w0, v0)
        s2 = sums(rows_own, rows_sib, w2, v2)
        return jnp.where(left, s0, s2), jnp.where(left, s2, s0)

    def end(rows_own, rows_sib, w3):
        return sums(rows_own, rows_sib, w3, swapped(w3))

    w2 = send(w1, ring, "ring_2")
    w1, token = fence(live[:1], w1)
    first, second, token = tie((first, second, token))
    rows_own = jnp.where(here, attended, first)
    rows_sib = jnp.where(here, first, second)
    s1 = region(token, begin, rows_own, rows_sib, w1)
    middle = to_owners(s1, (1, 1), "1")
    w2, s1 = tie((w2, s1))
    w3 = send(w0, back, "ring_after")
    low_sum, high_sum = region(token, mix, rows_own, rows_sib, w0, v0, w2)
    low_sum, high_sum, *middle = tie((low_sum, high_sum, *middle))
    early = to_owners(low_sum, (0, 2), "02") + to_owners(high_sum, (2, 0), "20")
    w3, low_sum, high_sum = tie((w3, low_sum, high_sum))
    s3 = region(token, end, rows_own, rows_sib, w3)
    middle += early
    last = to_owners(s3, (3, 3), "3")
    spot = jnp.reshape(y, (1,))
    base = finish(middle[::2], middle[1::2], residual_in, gate, spot)
    return finish(last[::2], last[1::2], base, gate, spot)


def solution(mesh):
    sizes = tuple(mesh.shape[axis] for axis in AXES)
    in_specs = (
        P(("groups", "frame"), ("head", "sub")),
        P(None, ("groups", "frame"), ("head", "sub")),
        P(("groups", "frame"), ("head", "sub")),
        P(("groups", "head", "sub")),
        P(("head", "sub"), "frame"),
        P(("groups", "frame"), None),
        P(("groups", "frame")),
    )
    return jax.shard_map(
        ringed if sizes == (2, 4, 2, 2) else plain,
        mesh=mesh,
        in_specs=in_specs,
        out_specs=P(("groups", "frame"), ("head", "sub")),
        check_vma=False,
    )
```

```python
import math

import jax
import jax.numpy as jnp
from jax import lax
from jax.experimental import pallas as pl
from jax.experimental.pallas import tpu as pltpu
from jax.sharding import PartitionSpec as P

HEAD_DIM = 128
TILES_F = 6
KSEL = 8
AXES = ("groups", "frame", "head", "sub")
MIB = 1 << 20


def weight(microseconds):
    return pl.CostEstimate(
        flops=int(microseconds * 1e9), bytes_accessed=int(microseconds * 3e6), transcendentals=0
    )


def fence_kernel(token, out):
    out[0] = token[0]


def fence(token, *arrays):
    *arrays, token = lax.optimization_barrier((*arrays, token))
    scalar = pl.BlockSpec(memory_space=pltpu.SMEM)
    token = pl.pallas_call(
        fence_kernel,
        out_shape=jax.ShapeDtypeStruct((1,), jnp.int32),
        in_specs=[scalar],
        out_specs=scalar,
        compiler_params=pltpu.CompilerParams(vmem_limit_bytes=MIB),
        cost_estimate=weight(50),
        name="fence",
    )(token)
    return (*arrays, token)


def attend_kernel(ids, live, q_ref, own_ref, low_ref, high_ref, out_ref, kv, sems):
    tiles = ids.shape[0]
    rows, width = q_ref.shape
    tile = rows // tiles
    heads = width // HEAD_DIM
    copies = [
        pltpu.make_async_copy(src, kv.at[:, pl.ds(i * rows, rows), :], sems.at[i])
        for i, src in enumerate((low_ref, own_ref, high_ref))
    ]
    for copy in copies:
        copy.start()
    for copy in copies:
        copy.wait()
    scale = math.log2(math.e) / math.sqrt(HEAD_DIM)
    key_row = lax.broadcasted_iota(jnp.int32, (KSEL * tile, 1), 0)
    lanes = [slice(h * HEAD_DIM, (h + 1) * HEAD_DIM) for h in range(heads)]

    def one_tile(t, carry):
        row = pl.multiple_of(t * tile, tile)
        starts = [pl.multiple_of(ids[t, s] * tile, tile) for s in range(KSEL)]

        def listed(which, lane):
            return jnp.concatenate([kv[which, pl.ds(s, tile), lane] for s in starts], axis=0)

        scores = jnp.concatenate(
            [
                lax.dot_general(
                    listed(0, lane),
                    q_ref[pl.ds(row, tile), lane],
                    (((1,), (1,)), ((), ())),
                    preferred_element_type=jnp.float32,
                )
                for lane in lanes
            ],
            axis=1,
        )
        scores = jnp.where(key_row < live[t] * tile, scores * scale, -1e30)
        expo = jnp.exp2(scores - jnp.max(scores, axis=0, keepdims=True))
        probs = (expo * (1.0 / jnp.sum(expo, axis=0, keepdims=True))).astype(jnp.bfloat16)
        for h, lane in enumerate(lanes):
            out_ref[pl.ds(row, tile), lane] = lax.dot_general(
                probs[:, h * tile : (h + 1) * tile],
                listed(1, lane),
                (((0,), (0,)), ((), ())),
                preferred_element_type=jnp.float32,
            ).astype(jnp.bfloat16)
        return carry

    lax.fori_loop(0, tiles, one_tile, 0)


def attend(queries, keyvals, low, high, pattern, live):
    rows, width = queries.shape
    tile_count = pattern.shape[0]
    local_ids = pattern - (lax.axis_index("frame") * tile_count - TILES_F)
    local_ids = jnp.clip(local_ids, 0, 3 * tile_count - 1)
    anywhere = pl.BlockSpec(memory_space=pl.ANY)
    scalars = pl.BlockSpec(memory_space=pltpu.SMEM)
    whole = pl.BlockSpec(memory_space=pltpu.VMEM)
    return pl.pallas_call(
        attend_kernel,
        out_shape=jax.ShapeDtypeStruct((rows, width), jnp.bfloat16),
        in_specs=[scalars, scalars, whole, anywhere, anywhere, anywhere],
        out_specs=whole,
        scratch_shapes=[
            pltpu.VMEM((2, 3 * rows, width), jnp.bfloat16),
            pltpu.SemaphoreType.DMA((3,)),
        ],
        compiler_params=pltpu.CompilerParams(vmem_limit_bytes=24 * MIB),
        cost_estimate=weight(8),
        name="attend",
    )(local_ids, live, queries, keyvals, low, high)


def halos(keyvals):
    count = lax.axis_size("frame")
    forward = [(i, i + 1) for i in range(count - 1)]
    backward = [(b, a) for a, b in forward]
    return lax.ppermute(keyvals, "frame", forward), lax.ppermute(keyvals, "frame", backward)


def plain(queries, keyvals, residual_in, gate, out_weight, pattern, live):
    low, high = halos(keyvals)
    attended = attend(queries, keyvals, low, high, pattern, live)
    weights = lax.all_gather(out_weight, "frame", axis=1, tiled=True)
    partial_rows = jnp.dot(attended, weights, preferred_element_type=jnp.float32)
    summed = lax.psum_scatter(
        partial_rows.astype(jnp.bfloat16), ("head", "sub"), scatter_dimension=1, tiled=True
    ).astype(jnp.float32)
    return residual_in + gate[None, :] * summed


def place(y, f, x, c):
    return ((y * 4 + f) * 2 + x) * 2 + c


def pairs(move, keep=lambda y, f, x, c: True):
    found = []
    for y in range(2):
        for f in range(4):
            for x in range(2):
                for c in range(2):
                    if keep(y, f, x, c):
                        found.append((place(y, f, x, c), place(*move(y, f, x, c))))
    return found


def block_at(k, f, x):
    return (f - k) % 4 if x == 0 else (f + k) % 4


def to_owner(steps, crosses):
    def move(y, f, x, c):
        g = block_at(steps[y ^ c][x], f, x)
        return c, f, g // 2, g % 2

    return pairs(move, lambda y, f, x, c: (y ^ c) in crosses)


def send(array, route, name):
    with jax.named_scope(name):
        return lax.ppermute(array, AXES, route)


def after(value, *earlier):
    return lax.optimization_barrier((value, *earlier))[0]


def finish_kernel(spot, *refs):
    residual, gate, out = refs[-3:]
    half = residual.shape[1] // 2
    count = (len(refs) - 3) // 2
    for cross, parts in ((0, refs[:count]), (1, refs[count : 2 * count])):
        lanes = pl.ds(pl.multiple_of((spot[0] ^ cross) * half, half), half)
        total = parts[0][...].astype(jnp.float32)
        for part in parts[1:]:
            total = total + part[...].astype(jnp.float32)
        out[:, lanes] = residual[:, lanes] + gate[:, lanes] * total


def finish(direct, crossed, residual_in, gate, spot):
    rows, width = residual_in.shape
    step = rows // 2
    parts = [pl.BlockSpec((step, part.shape[1]), lambda i: (i, 0)) for part in direct + crossed]
    wide = pl.BlockSpec((step, width), lambda i: (i, 0))
    return pl.pallas_call(
        finish_kernel,
        grid=(rows // step,),
        out_shape=jax.ShapeDtypeStruct((rows, width), jnp.float32),
        in_specs=[pl.BlockSpec(memory_space=pltpu.SMEM)]
        + parts
        + [wide, pl.BlockSpec((1, width), lambda i: (0, 0))],
        out_specs=wide,
        compiler_params=pltpu.CompilerParams(vmem_limit_bytes=24 * MIB),
        name="finish",
    )(spot, *direct, *crossed, residual_in, gate[None, :])


def ringed(queries, keyvals, residual_in, gate, out_weight, pattern, live):
    y = lax.axis_index("groups")
    x = lax.axis_index("head")
    c = lax.axis_index("sub")
    half = out_weight.shape[1] // 2
    tie = lax.optimization_barrier

    ring = pairs(lambda y, f, x, c: (y, (f + 1) % 4 if x == 0 else (f - 1) % 4, x, c))
    back = [(target, source) for source, target in ring]
    sibling = pairs(lambda y, f, x, c: (y, f, x, 1 - c))
    here = y == c
    left = x == 0

    def to_owners(array, steps, name):
        return [
            send(array, to_owner((steps,) * 2, (0,)), "sums_" + name),
            send(array, to_owner((steps,) * 2, (1,)), "sums_cross_" + name),
        ]

    low, high = halos(keyvals)
    w0 = lax.dynamic_slice_in_dim(out_weight, y * half, half, axis=1)
    v0 = send(w0, sibling, "core_swap_0")
    w0, low = tie((w0, low))
    w1 = send(w0, ring, "ring_1")
    attended = attend(queries, keyvals, low, high, pattern, live)
    first = send(
        attended,
        pairs(lambda y, f, x, c: (1 - y, f, x, c) if c == y else (y, f, x, 1 - c)),
        "rows_1",
    )
    second = send(
        attended,
        pairs(lambda y, f, x, c: (1 - y, f, x, 1 - c), lambda y, f, x, c: c != y),
        "rows_2",
    )

    def region(token, body, *operands):
        shapes = jax.eval_shape(body, *operands)
        return lax.cond(
            token[0] > 0,
            body,
            lambda *_: jax.tree.map(lambda leaf: jnp.zeros(leaf.shape, leaf.dtype), shapes),
            *operands,
        )

    def sums(rows_own, rows_sib, own, sib):
        total = jnp.dot(rows_own, own, preferred_element_type=jnp.float32)
        total = total + jnp.dot(rows_sib, sib, preferred_element_type=jnp.float32)
        return total.astype(jnp.bfloat16)

    def swapped(w):
        return send(w, sibling, "core_swap")

    def begin(rows_own, rows_sib, w1):
        return sums(rows_own, rows_sib, w1, swapped(w1))

    def mix(rows_own, rows_sib, w0, v0, w2):
        v2 = swapped(w2)
        s0 = sums(rows_own, rows_sib, w0, v0)
        s2 = sums(rows_own, rows_sib, w2, v2)
        return jnp.where(left, s0, s2), jnp.where(left, s2, s0)

    def end(rows_own, rows_sib, w3):
        return sums(rows_own, rows_sib, w3, swapped(w3))

    w2 = send(w1, ring, "ring_2")
    w1, token = fence(live[:1], w1)
    first, second, token = tie((first, second, token))
    rows_own = jnp.where(here, attended, first)
    rows_sib = jnp.where(here, first, second)
    s1 = region(token, begin, rows_own, rows_sib, w1)
    middle = to_owners(s1, (1, 1), "1")
    w3 = send(w0, back, "ring_after")
    low_sum, high_sum = region(token, mix, rows_own, rows_sib, w0, v0, w2)
    low_sum, high_sum, *middle = tie((low_sum, high_sum, *middle))
    early = to_owners(low_sum, (0, 2), "02") + to_owners(high_sum, (2, 0), "20")
    w3, low_sum, high_sum = tie((w3, low_sum, high_sum))
    s3 = region(token, end, rows_own, rows_sib, w3)
    middle += early
    last = to_owners(s3, (3, 3), "3")
    spot = jnp.reshape(y, (1,))
    base = finish(middle[::2], middle[1::2], residual_in, gate, spot)
    return finish(last[::2], last[1::2], base, gate, spot)


def solution(mesh):
    sizes = tuple(mesh.shape[axis] for axis in AXES)
    in_specs = (
        P(("groups", "frame"), ("head", "sub")),
        P(None, ("groups", "frame"), ("head", "sub")),
        P(("groups", "frame"), ("head", "sub")),
        P(("groups", "head", "sub")),
        P(("head", "sub"), "frame"),
        P(("groups", "frame"), None),
        P(("groups", "frame")),
    )
    return jax.shard_map(
        ringed if sizes == (2, 4, 2, 2) else plain,
        mesh=mesh,
        in_specs=in_specs,
        out_specs=P(("groups", "frame"), ("head", "sub")),
        check_vma=False,
    )
```
